512 devices in a mesh: dp: 32 (over y, x, core), owner: 16 (over z).
Axes of the slice: x: 4, y: 4, z: 16, core: 2. Of those that a mesh axis runs over, the one named last changes fastest.
Arguments:
- partials: float32 [32, 256, 256, 256], P('dp', None, 'owner'), may hold values from -0.125 to 0.125
- statistics: float32 [256, 2, 256, 256], P('dp', None, 'owner'), may hold values from -250 to 250, as said below
- assignment: int32 [512, 1], replicated, may hold values from 0 to 15; in each aligned block of 16 rows (0 to 15, 16 to 31, ...) at most 2 rows name the same one
Outputs:
- preconditioned: float32 [256, 256, 256], P('dp', 'owner')
- new_statistics: float32 [256, 2, 256, 256], P('dp', None, 'owner')
- stored_roots: bfloat16 [32, 16, 2, 256, 256], P('dp', 'owner')
The draws below stay inside these ranges and needn't reach their ends.
Inputs may be any that keep to these rules, and one draw needn't show every extreme that they name: `assignment`: among the 16 matrices of one dp index (rows 16 k to 16 k + 15) no root owner appears more than 2 times, and 2 is reached in some dp index; every root owner appears somewhere. Every matrix statistics[b, k] is symmetric positive definite.
All inputs are finite; a program needn't handle non-finite values.
Results may differ from the reference program's by a relative error of at most 0.0014.
Values may be sent and summed in bfloat16 or wider, within the bound.
A program may use at most 128 MiB of HBM per device.

```python
import math
import jax
import jax.numpy as jnp
import numpy as np
from jax import lax

BS = 256
ITERS = 7
NB = 256
SPD = 16
CAP = 2
NSTAT = 512
N_DP = 32
N_OWNER = 16


def draw_statistics(key, part):
    key = jax.random.fold_in(key, 7)
    first = jax.random.fold_in(key, 0)
    third = jax.random.fold_in(key, 2)
    fourth = jax.random.fold_in(key, 3)
    upper_scale = 3.0
    limit = 1.7320508
    base = jax.random.uniform(first, (NB, 2, BS, BS), jnp.float32, -limit, limit)
    mixed = base
    scales = jnp.exp(jax.random.uniform(third, (NB, 2, BS), jnp.float32, jnp.log(0.3), jnp.log(upper_scale)))
    diagonal = jnp.exp(jax.random.uniform(fourth, (NB, 2, BS), jnp.float32, jnp.log(0.05), jnp.log(0.5)))
    gram = jnp.einsum('bkij,bklj->bkil', mixed, mixed, precision=lax.Precision.HIGHEST) / BS
    gram = 0.5 * (gram + jnp.swapaxes(gram, 2, 3))
    unit_matrix = jnp.eye(BS, dtype=jnp.float32)
    matrix = gram * scales[:, :, :, None] * scales[:, :, None, :] + diagonal[:, :, :, None] * unit_matrix
    return matrix


def strengthened(entries, stream_key, source, target, blocks, factor):
    owner, partner = [(jnp.arange(entries.shape[axis_at]) // (entries.shape[axis_at] // blocks)).reshape([-1 if axis == axis_at else 1 for axis in range(entries.ndim)]) for axis_at in (source, target)]
    chosen = jax.random.permutation(stream_key, blocks)[partner]
    strong = (owner == chosen) | (owner == (partner + blocks // 2) % blocks)
    return jnp.where(strong, factor * entries, entries)


def steps_of(key, shape, pieces, smallest, high):
    gain = 1.0
    for axis_at, blocks in pieces:
        heights = jax.random.uniform(jax.random.fold_in(jax.random.fold_in(key, 6), axis_at), (blocks,), jnp.float32, smallest / len(pieces), high / len(pieces))
        gain = gain * jnp.repeat(jnp.exp(heights), shape[axis_at] // blocks).reshape((-1,) + (1,) * (len(shape) - 1 - axis_at))
    return gain


def deal_out(stream_key, own, number, rows, number_of, top, most, slope):
    sequence = jax.random.permutation(stream_key, number_of)
    heavy_load, ordinary = load_shares(number_of, rows * top, most, slope, True), load_shares(number_of, rows * top, most, slope, False)
    places = jnp.arange(number_of)

    def named(tallies, turn):
        used = int((tallies > 0).sum())
        fixed = max(1, used // 4)
        shifted = fixed + (places - fixed + turn * (used - fixed)) % max(1, number_of - fixed)
        return jnp.zeros((number_of,), jnp.int32).at[sequence[jnp.where(places < fixed, places, shifted)]].set(jnp.asarray(tallies, jnp.int32))

    tallies = jnp.where(number % 4 == 0, named(heavy_load, number // 4), named(ordinary, number - number // 4 - 1))
    mixed = jax.random.permutation(jax.random.fold_in(own, 3), number_of)
    source_of, receiver = mixed[0:number_of // 2 * 2:2], mixed[1:number_of // 2 * 2:2]
    slack = jnp.minimum(tallies[source_of] - 1, most - tallies[receiver]) // 2
    slack = jnp.where((source_of == sequence[0]) | (receiver == sequence[0]) | (tallies[receiver] == 0), 0, jnp.maximum(slack, 0))
    shifted = jax.random.randint(jax.random.fold_in(own, 4), (number_of // 2,), 0, 1 << 20) % (slack + 1)
    tallies = tallies.at[source_of].add(-shifted).at[receiver].add(shifted)
    items = jnp.searchsorted(jnp.cumsum(tallies), jnp.arange(rows * top), side="right").astype(jnp.int32)
    listing = items.reshape(top, rows).T
    listing = listing[jax.random.permutation(jax.random.fold_in(own, 1), rows)]
    turn = jax.random.randint(jax.random.fold_in(own, 2), (rows, 1), 0, top)
    return jnp.take_along_axis(listing, (jnp.arange(top)[None, :] + turn) % top, axis=1)


def load_shares(amount, total, reach, lean, full):
    weights = [(1 << 20) // math.isqrt(standing ** lean) + 1 for standing in range(1, amount + 1)]
    largest = reach if full else min(reach, max(-(-total // amount), total * weights[0] // sum(weights)))
    least = 1 if total - largest >= amount - 1 else 0
    given, spare = [largest] + [least] * (amount - 1), total - largest - least * (amount - 1)
    while spare > 0:
        movable = [i for i in range(1, amount) if given[i] < largest] or [i for i in range(1, amount) if given[i] < reach]
        whole, remaining = sum([weights[i] for i in movable]), spare
        for i in movable:
            more = min(reach - given[i], max(1, remaining * weights[i] // whole), spare)
            given[i] = given[i] + more
            spare = spare - more
    return np.array(given)


def noise_with(stream_key, extent, spread, most, shards, heavy, held_as=jnp.bfloat16):
    values = spread * jax.random.normal(stream_key, extent, jnp.float32)
    if shards:
        values = values * steps_of(stream_key, extent, shards, -0.22, 0.18)
    return jnp.clip(strengthened(values, jax.random.fold_in(stream_key, 3), *heavy), -most, most).astype(held_as)


def setup_inputs(seed: int = 0) -> dict:
    seeds = jax.random.split(jax.random.key(seed), 4)
    partials = noise_with(seeds[0], (N_DP, NB, BS, BS), (BS * N_DP) ** -0.5, 0.125, ((0, 32), (2, 16)), (0, 1, 32, 2.75), jnp.float32)
    statistics = draw_statistics(jax.random.fold_in(seeds[3], 71), 0)
    assignment_keys = jax.random.split(jax.random.fold_in(seeds[2], 1), NSTAT // SPD)
    assignment_turns = jax.random.permutation(jax.random.fold_in(seeds[2], 3), NSTAT // SPD)
    assignment = jax.vmap(lambda own, number: deal_out(jax.random.fold_in(seeds[2], 2), own, number, SPD, N_OWNER, 1, CAP, 2))(assignment_keys, assignment_turns).reshape((NSTAT, 1))
    return dict(partials=partials, statistics=statistics, assignment=assignment)


def batched(first, second):
    return jnp.einsum('nij,njk->nik', first, second, precision=lax.Precision.HIGHEST)

def inverse_root(matrices):
    order = matrices.shape[-1]
    unit_matrix = jnp.eye(order, dtype=jnp.float32)
    magnitude = jnp.sqrt(lax.optimization_barrier(jnp.sum(matrices * matrices, axis=(1, 2))) + 1e-06)[:, None, None]
    current = matrices / magnitude
    result = current
    for iteration in range(ITERS):
        factor = (5.0 * unit_matrix - current) * 0.25
        if iteration == 0:
            result = factor * magnitude ** (-0.25)
        else:
            result = batched(result, factor)
        if iteration + 1 < ITERS:
            square = batched(factor, factor)
            current = batched(batched(square, square), current)
    return result

def reference(partials, statistics, assignment):
    grad = lax.optimization_barrier(jnp.sum(partials, axis=0))
    left_new = statistics[:, 0] + jnp.einsum('brk,bsk->brs', grad, grad, precision=lax.Precision.HIGHEST)
    right_new = statistics[:, 1] + jnp.einsum('bkr,bks->brs', grad, grad, precision=lax.Precision.HIGHEST)
    new_statistics = jnp.stack([left_new, right_new], axis=1)
    roots = inverse_root(statistics.reshape(NSTAT, BS, BS))
    left_roots = roots[0::2]
    right_roots = roots[1::2]
    shaped = batched(left_roots, grad)
    preconditioned = batched(shaped, right_roots)
    owner_list = assignment[:, 0].astype(jnp.int32)
    positions = jnp.arange(NSTAT, dtype=jnp.int32)
    groups = positions // SPD
    earlier = (groups[:, None] == groups[None, :]) & (owner_list[:, None] == owner_list[None, :]) & (positions[:, None] < positions[None, :])
    ranks = lax.optimization_barrier(jnp.sum(earlier.astype(jnp.int32), axis=0))
    target = ((groups * N_OWNER + owner_list) * CAP + ranks).astype(jnp.int32)
    stored = jnp.zeros((N_DP * N_OWNER * CAP, BS, BS), jnp.float32).at[target].set(roots)
    stored_roots = stored.reshape(N_DP, N_OWNER, CAP, BS, BS).astype(jnp.bfloat16)
    return (preconditioned, new_statistics, stored_roots)
```

```python
import jax
import jax.numpy as jnp
from jax import lax
from jax.experimental import pallas as pl
from jax.experimental.pallas import tpu as pltpu
from jax.sharding import PartitionSpec as P

MESH = pl.DeviceIdType.MESH
F32, BF16, I16, I32 = jnp.float32, jnp.bfloat16, jnp.int16, jnp.int32
NX = NY = 4
NZ = 16
NB = 8
ROWS = 16
N = 256
H = 128
ITERS = 7
LEVELS = 32760.0 / 32768.0
B_MSG, C_MSG, G_MSG, R_MSG = 33, 9, 17, 25
G_PARTS = ((0, 9), (9, 8))
R_PARTS = ((0, 13), (13, 12))


def code(x):
    return jnp.round(x).astype(I32).astype(I16)


def encode(x, dst):
    m = x.shape[0]
    left, right = x[:, :, :H], x[:, :, H:]
    top = jnp.maximum(jnp.max(jnp.abs(left), axis=0), jnp.max(jnp.abs(right), axis=0))
    e = jnp.ceil(jnp.log2(jnp.maximum(top, 1e-30)))
    up = (jnp.exp2(15.0 - e) * LEVELS)[None]
    dst[0:m] = code(left * up)
    dst[m : 2 * m] = code(right * up)
    dst[2 * m] = code(e)


def value(q):
    return q.astype(I32).astype(F32)


def unit(e):
    return jnp.exp2(value(e) - 15.0) * (1.0 / LEVELS)


def decode(src, m):
    down = unit(src[2 * m])[None]
    return value(src[0:m]) * down, value(src[m : 2 * m]) * down


def encode_root(x, dst):
    x = jnp.concatenate([x[:H, :H], x[:H, H:], x[H:, H:]], axis=0).reshape(24, ROWS, H)
    e = jnp.ceil(jnp.log2(jnp.maximum(jnp.max(jnp.abs(x), axis=0), 1e-30)))
    dst[0:24] = code(x * (jnp.exp2(15.0 - e) * LEVELS)[None])
    dst[24] = code(e)


def decode_root(q):
    v = (value(q[0:24]) * unit(q[24])[None]).reshape(3 * H, H)
    return v[:H], v[H : 2 * H], v[2 * H :]


def split(x):
    high = x.astype(BF16)
    return high, (x - high.astype(F32)).astype(BF16)


def dot(a, b):
    return jnp.dot(a, b, preferred_element_type=F32)


def dot_nt(a, b):
    return lax.dot_general(a, b, (((1,), (1,)), ((), ())), preferred_element_type=F32)


def dot3(a, b):
    (ah, al), (bh, bl) = a, b
    return dot(ah, bh) + (dot(al, bh) + dot(ah, bl))


def kernel(
    p_ref, s_ref, owner_ref, pre_ref, new_ref, kept_ref,
    srows, own, other, bsend, brecv, csend, crecv, acc, gown, smat, cur, root, gq, ghi, glo, rq,
    own_sem, stat_sem, a_send, a_recv, b_send, b_recv, c_send, c_recv, s_send, s_recv,
    g_right, g_left, g_recv, r_right, r_left, r_recv,
):
    dp = lax.axis_index("dp")
    z = lax.axis_index("owner")
    core = lax.rem(dp, 2)
    x = lax.rem(dp // 2, NX)
    y = dp // (2 * NX)

    def plane(yy, xx, cc):
        return ((yy * NX + xx) * 2 + cc, z)

    def column(zz):
        return (dp, zz)

    def step(i, k, n):
        return lax.rem(i + k, n)

    partner = plane(y, x, 1 - core)

    def along(half, k):
        return plane(y, step(x, k, NX), core) if half == 0 else plane(step(y, k, NY), x, core)

    barrier = pltpu.get_barrier_semaphore()
    for k in range(1, NZ):
        pl.semaphore_signal(barrier, inc=1, device_id=column(step(z, k, NZ)), device_id_type=MESH)
    pl.semaphore_signal(barrier, inc=1, device_id=partner, device_id_type=MESH)
    for half in range(2):
        for k in range(1, 4):
            pl.semaphore_signal(barrier, inc=1, device_id=along(half, k), device_id_type=MESH)
    pl.semaphore_wait(barrier, NZ - 1 + 1 + 6)

    def remote(src, dst, send, recv, to):
        return pltpu.make_async_remote_copy(
            src_ref=src, dst_ref=dst, send_sem=send, recv_sem=recv, device_id=to, device_id_type=MESH
        )

    def chunk(half, k, cc):
        if half == 0:
            return p_ref.at[:, step(x, k, NX), cc, pl.ds(0, 4)]
        return p_ref.at[step(y, k, NY), :, cc, pl.ds(4, 4)]

    def to_partner(half, k):
        return remote(
            chunk(half, k, 1 - core), other.at[half, k], a_send.at[half, k], a_recv.at[half, k], partner
        )

    def mine(half, k):
        return pltpu.make_async_copy(chunk(half, k, core), own.at[half, k], own_sem.at[half, k])

    def rows_to(k):
        to = step(z, k, NZ)
        return remote(s_ref.at[to], smat.at[z], s_send.at[k], s_recv.at[k], column(to))

    def rows_from(k):
        return remote(s_ref.at[z], smat.at[step(z, NZ - k, NZ)], s_send.at[k], s_recv.at[k], column(step(z, k, NZ)))

    ORDER = (2, 1, 3, 0)
    for half in range(2):
        to_partner(half, 2).start()
        mine(half, 2).start()
    for k in (8, 7, 9, 6, 10, 5, 11, 4, 12, 3, 13, 2, 14, 1, 15):
        rows_to(k).start()
    for k in ORDER[1:]:
        for half in range(2):
            to_partner(half, k).start()
            mine(half, k).start()
    own_rows = pltpu.make_async_copy(s_ref.at[z], smat.at[z], s_recv.at[0])
    own_rows.start()
    all_rows = pltpu.make_async_copy(s_ref, srows, stat_sem)
    all_rows.start()

    def b_copy(half, k):
        return remote(bsend.at[half, k - 1], brecv.at[half, k - 1], b_send.at[half, k - 1], b_recv.at[half, k - 1], along(half, k))

    def c_copy(half, k):
        return remote(csend.at[half, k - 1], crecv.at[half, k - 1], c_send.at[half, k - 1], c_recv.at[half, k - 1], along(1 - half, k))

    for k in ORDER:
        for half in range(2):
            to_partner(half, k).wait_recv()
            mine(half, k).wait()
            total = own[half, k] + other[half, k]
            if k:
                encode(total.reshape(16, ROWS, N), bsend.at[half, k - 1])
                b_copy(half, k).start()
            else:
                acc[half] = total

    right_z, left_z = column(step(z, 1, NZ)), column(step(z, NZ - 1, NZ))

    def ring(buf, parts, right_sem, left_sem, recv):
        def hop(d, s, p):
            origin = step(z, NZ - s, NZ) if d == 0 else step(z, s, NZ)
            at = buf.at[origin, pl.ds(*parts[p])]
            sem = (right_sem if d == 0 else left_sem).at[s, p]
            return remote(at, at, sem, recv.at[origin, p], right_z if d == 0 else left_z)

        def arrive(d, s, p, forward):
            c = hop(d, s, p)
            c.wait_recv()
            if forward:
                c.start()

        def begin():
            for p in range(2):
                for d in range(2):
                    hop(d, 0, p).start()

        def finish():
            for p in range(2):
                for s in range(8):
                    hop(0, s, p).wait_send()
                for s in range(7):
                    hop(1, s, p).wait_send()

        return arrive, begin, finish

    g_arrive, g_begin, g_finish = ring(gq, G_PARTS, g_right, g_left, g_recv)
    r_arrive, r_begin, r_finish = ring(rq, R_PARTS, r_right, r_left, r_recv)

    def unpack_g(origin):
        a, b = decode(gq.at[origin], NB)
        ah, al = split(a)
        bh, bl = split(b)
        ghi[origin, :, :, :H] = ah
        ghi[origin, :, :, H:] = bh
        glo[origin, :, :, :H] = al
        glo[origin, :, :, H:] = bl

    def plane_sums():
        for half in range(2):
            left = acc[half, :, :, :, :H].reshape(16, ROWS, H)
            right = acc[half, :, :, :, H:].reshape(16, ROWS, H)
            for k in (1, 3, 2):
                b_copy(half, k).wait_recv()
                a, b = decode(brecv.at[half, k - 1], 16)
                left, right = left + a, right + b
            acc[half, :, :, :, :H] = left.reshape(4, 4, ROWS, H)
            acc[half, :, :, :, H:] = right.reshape(4, 4, ROWS, H)
            me = y if half == 0 else x
            for k in (2, 1, 3):
                encode(acc[half, step(me, k, 4)], csend.at[half, k - 1])
                c_copy(half, k).start()


    def own_sums():
        for half in range(2):
            me = y if half == 0 else x
            g = acc[half, me]
            left, right = g[:, :, :H], g[:, :, H:]
            for k in (1, 3, 2):
                c_copy(half, k).wait_recv()
                a, b = decode(crecv.at[half, k - 1], 4)
                left, right = left + a, right + b
            gown[pl.ds(4 * half, 4), :, :H] = left
            gown[pl.ds(4 * half, 4), :, H:] = right

    def unpack_g(origin):
        a, b = decode(gq.at[origin], NB)
        ah, al = split(a)
        bh, bl = split(b)
        ghi[origin, :, :, :H] = ah
        ghi[origin, :, :, H:] = bh
        glo[origin, :, :, :H] = al
        glo[origin, :, :, H:] = bl

    def g_step(s):
        for p in range(2):
            g_arrive(0, s, p, s < 8)
            if s < 8:
                g_arrive(1, s, p, s < 7)

    def unpack_step(s):
        unpack_g(step(z, NZ - s, NZ))
        if s < 8:
            unpack_g(step(z, s, NZ))

    def iteration():
        current = cur[...]
        f = factor_of(current)
        fs, rs = split(f), split(root[...])
        both = tuple(jnp.concatenate([u, v], axis=0) for u, v in zip(fs, rs))
        product = dot3(both, fs)
        root[...] = product[N:]
        cur[...] = powered(fs, product[:N], current)

    own_rows.wait()
    for k in range(1, NZ):
        rows_from(k).wait_recv()
    eye = (lax.broadcasted_iota(I32, (N, N), 0) == lax.broadcasted_iota(I32, (N, N), 1)).astype(F32)

    def factor_of(current):
        return (5.0 * eye - current) * 0.25

    def powered(f, square, current):
        s = split(square)
        q = dot3(s, s)
        return dot3(split(q), split(current))

    matrix = smat[...].reshape(N, N)
    magnitude = jnp.sqrt(jnp.sum(matrix * matrix, keepdims=True) + 1e-6)
    current = matrix / magnitude
    f = factor_of(current)
    root[...] = f * lax.rsqrt(jnp.sqrt(magnitude))
    fs = split(f)
    cur[...] = powered(fs, dot3(fs, fs), current)

    plane_sums()
    iteration()
    own_sums()
    encode(gown[...], gq.at[z])
    g_begin()
    iteration()
    iteration()
    g_step(1)
    iteration()
    g_step(2)
    iteration()
    last = dot3(split(root[...]), split(factor_of(cur[...])))
    encode_root(last, rq.at[z])
    r_begin()

    def r_step(s, *units):
        units = units + (None,) * 4
        for i, (p, d) in enumerate(((0, 0), (0, 1), (1, 0), (1, 1))):
            if s < 8 or d == 0:
                r_arrive(d, s, p, s < 8 - d)
            if units[i] is not None:
                units[i]()

    unpack_g(z)
    unpack_step(1)
    for s in range(1, 4):
        g_step(2 * s + 1)
        unpack_step(2 * s)
        r_step(s)
        g_step(2 * s + 2)
        unpack_step(2 * s + 1)
    unpack_step(8)
    all_rows.wait()

    pick = (
        lax.broadcasted_iota(I32, (ROWS, N), 1) == lax.broadcasted_iota(I32, (ROWS, N), 0) + z * ROWS
    ).astype(F32).astype(BF16)

    def halves(b):
        return ghi[:, b].reshape(N, N), glo[:, b].reshape(N, N)

    def statistics(b):
        gh, gl = halves(b)
        rh, rl = split(gown[b])
        one = dot_nt(jnp.concatenate([rh, rl, pick], axis=0), gh)
        two = dot_nt(jnp.concatenate([rh, pick], axis=0), gl)
        new_ref[2 * b] = srows[2 * b] + one[:16] + (one[16:32] + two[:16])
        ch, cl = one[32:48].astype(BF16), two[16:32].astype(BF16)
        three = dot(jnp.concatenate([ch, cl], axis=0), gh)
        new_ref[2 * b + 1] = srows[2 * b + 1] + three[:16] + (three[16:32] + dot(ch, gl))

    pick_low = (
        lax.broadcasted_iota(I32, (ROWS, H), 1)
        == lax.broadcasted_iota(I32, (ROWS, H), 0) + (z - 8) * ROWS
    ).astype(F32).astype(BF16)

    def precondition(t):
        b = step(pair, t, NB)
        gh, gl = halves(b)
        q = rq[2 * b]
        down = unit(q[24])
        bh, bl = split((value(q[8:16]) * down[None]).reshape(H, H))
        upper = value(rq[2 * b, lax.rem(z, 8)]) * down
        lower = dot_nt(pick_low, bh) + dot_nt(pick_low, bl)
        rows = jnp.concatenate([jnp.where(z < 8, upper, lower), value(rq[2 * b, 8 + z]) * down], axis=1)
        lh, ll = split(rows)
        shaped = dot(jnp.concatenate([lh, ll], axis=0), gh)
        shaped = shaped[:16] + (shaped[16:] + dot(lh, gl))
        a, c, d = decode_root(rq[2 * b + 1])
        right = jnp.concatenate(
            [jnp.concatenate([a, c], axis=1), jnp.concatenate([c.T, d], axis=1)], axis=0
        )
        rh, rl = split(right)
        sh, sl = split(shaped)
        out = dot(jnp.concatenate([sh, sl], axis=0), rh)
        pre_ref[b] = out[:16] + (out[16:] + dot(sh, rl))

    pair = z // 2

    def stat(b):
        return lambda: statistics(b)

    def pre(t):
        return lambda: precondition(t)

    r_step(4, stat(0), stat(1), pre(0), stat(2))
    r_step(5, stat(3), pre(1), stat(4), pre(7))
    r_step(6, stat(5), pre(2), stat(6), pre(6))
    r_step(7, stat(7))
    r_step(8, pre(3), None, pre(5))
    precondition(4)

    first, second, count = jnp.int32(0), jnp.int32(0), jnp.int32(0)
    for j in range(16):
        hit = owner_ref[dp * 16 + j] == z
        first = jnp.where(hit & (count == 0), j, first)
        second = jnp.where(hit & (count == 1), j, second)
        count = count + hit.astype(I32)
    for slot, j in enumerate((first, second)):
        live = (count > slot).astype(F32)
        a, c, d = decode_root(rq[j])
        kept_ref[slot, 0:8, :, :H] = (a * live).astype(BF16).reshape(8, ROWS, H)
        kept_ref[slot, 0:8, :, H:] = (c * live).astype(BF16).reshape(8, ROWS, H)
        kept_ref[slot, 8:16, :, :H] = (c.T * live).astype(BF16).reshape(8, ROWS, H)
        kept_ref[slot, 8:16, :, H:] = (d * live).astype(BF16).reshape(8, ROWS, H)

    for half in range(2):
        for k in range(4):
            to_partner(half, k).wait_send()
        for k in range(1, 4):
            b_copy(half, k).wait_send()
            c_copy(half, k).wait_send()
    for k in range(1, NZ):
        rows_to(k).wait_send()
    g_finish()
    r_finish()


def shards(partials, statistics, assignment):
    vmem, dma = pltpu.VMEM, pltpu.SemaphoreType.DMA
    pre, new, kept = pl.pallas_call(
        kernel,
        out_shape=(
            jax.ShapeDtypeStruct((NB, ROWS, N), F32),
            jax.ShapeDtypeStruct((2 * NB, ROWS, N), F32),
            jax.ShapeDtypeStruct((2, 16, 16, N), BF16),
        ),
        in_specs=[
            pl.BlockSpec(memory_space=pl.ANY),
            pl.BlockSpec(memory_space=pl.ANY),
            pl.BlockSpec(memory_space=pltpu.SMEM),
        ],
        out_specs=[pl.BlockSpec(memory_space=pltpu.VMEM)] * 3,
        scratch_shapes=[
            vmem((2 * NB, ROWS, N), F32),
            vmem((2, 4, 4, 4, ROWS, N), F32),
            vmem((2, 4, 4, 4, ROWS, N), F32),
            vmem((2, 3, B_MSG, ROWS, H), I16),
            vmem((2, 3, B_MSG, ROWS, H), I16),
            vmem((2, 3, C_MSG, ROWS, H), I16),
            vmem((2, 3, C_MSG, ROWS, H), I16),
            vmem((2, 4, 4, ROWS, N), F32),
            vmem((NB, ROWS, N), F32),
            vmem((NZ, ROWS, N), F32),
            vmem((N, N), F32),
            vmem((N, N), F32),
            vmem((NZ, G_MSG, ROWS, H), I16),
            vmem((NZ, NB, ROWS, N), BF16),
            vmem((NZ, NB, ROWS, N), BF16),
            vmem((NZ, R_MSG, ROWS, H), I16),
            dma((2, 4)), dma, dma((2, 4)), dma((2, 4)),
            dma((2, 3)), dma((2, 3)), dma((2, 3)), dma((2, 3)),
            dma((NZ,)), dma((NZ,)),
            dma((8, 2)), dma((7, 2)), dma((NZ, 2)),
            dma((8, 2)), dma((7, 2)), dma((NZ, 2)),
        ],
        compiler_params=pltpu.CompilerParams(
            collective_id=0, has_side_effects=True, vmem_limit_bytes=60 * 1024 * 1024
        ),
        cost_estimate=pl.CostEstimate(flops=3_000_000_000, bytes_accessed=6_000_000, transcendentals=0),
    )(
        partials.reshape(NY, NX, 2, NB, ROWS, N),
        statistics.reshape(2 * NB, ROWS, N),
        assignment.reshape(-1),
    )
    return pre, new.reshape(NB, 2, ROWS, N), kept.reshape(1, 1, 2, N, N)


def solution(mesh):
    placed = (P("dp", None, "owner", None), P("dp", None, "owner", None), P())
    return jax.shard_map(
        shards,
        mesh=mesh,
        in_specs=placed,
        out_specs=(
            P("dp", "owner", None),
            P("dp", None, "owner", None),
            P("dp", "owner", None, None, None),
        ),
        check_vma=False,
    )
```

```python
import jax
import jax.numpy as jnp
from jax import lax
from jax.experimental import pallas as pl
from jax.experimental.pallas import tpu as pltpu
from jax.sharding import PartitionSpec as P

MESH = pl.DeviceIdType.MESH
F32, BF16, I16, I32 = jnp.float32, jnp.bfloat16, jnp.int16, jnp.int32
NX = NY = 4
NZ = 16
NB = 8
ROWS = 16
N = 256
H = 128
ITERS = 7
LEVELS = 32760.0 / 32768.0
A_MSG, B_MSG, C_MSG, G_MSG, R_MSG = 33, 17, 9, 17, 25
G_PARTS = ((0, 9), (9, 8))
R_PARTS = ((0, 13), (13, 12))


def code(x):
    return jnp.round(x).astype(I32).astype(I16)


def encode(halves, dst):
    left, right = halves
    m = left.shape[0]
    top = jnp.maximum(jnp.max(jnp.abs(left), axis=0), jnp.max(jnp.abs(right), axis=0))
    e = jnp.ceil(jnp.log2(jnp.maximum(top, 1e-30)))
    up = (jnp.exp2(15.0 - e) * LEVELS)[None]
    dst[0:m] = code(left * up)
    dst[m : 2 * m] = code(right * up)
    dst[2 * m] = code(e)


def value(q):
    return q.astype(I32).astype(F32)


def unit(e):
    return jnp.exp2(value(e) - 15.0) * (1.0 / LEVELS)


def decode(src, m):
    down = unit(src[2 * m])[None]
    return value(src[0:m]) * down, value(src[m : 2 * m]) * down


def encode_root(x, dst):
    x = jnp.concatenate([x[:H, :H], x[:H, H:], x[H:, H:]], axis=0).reshape(24, ROWS, H)
    e = jnp.ceil(jnp.log2(jnp.maximum(jnp.max(jnp.abs(x), axis=0), 1e-30)))
    dst[0:24] = code(x * (jnp.exp2(15.0 - e) * LEVELS)[None])
    dst[24] = code(e)


def decode_root(q):
    v = (value(q[0:24]) * unit(q[24])[None]).reshape(3 * H, H)
    return v[:H], v[H : 2 * H], v[2 * H :]


def split(x):
    high = x.astype(BF16)
    return high, (x - high.astype(F32)).astype(BF16)


def dot(a, b):
    return jnp.dot(a, b, preferred_element_type=F32)


def dot_nt(a, b):
    return lax.dot_general(a, b, (((1,), (1,)), ((), ())), preferred_element_type=F32)


def dot3(a, b):
    (ah, al), (bh, bl) = a, b
    return dot(ah, bh) + (dot(al, bh) + dot(ah, bl))


def kernel(
    p_ref, s_ref, pre_ref, new_ref, rq,
    srows, own, theirs, asend, arecv, bsend, brecv, csend, crecv, gown, smat, cur, root, gq, ghi, glo,
    own_sem, their_sem, stat_sem, a_send, a_recv, b_send, b_recv, c_send, c_recv, s_send, s_recv,
    g_right, g_left, g_recv, r_right, r_left, r_recv,
):
    dp = lax.axis_index("dp")
    z = lax.axis_index("owner")
    core = lax.rem(dp, 2)
    x = lax.rem(dp // 2, NX)
    y = dp // (2 * NX)

    def plane(yy, xx, cc):
        return ((yy * NX + xx) * 2 + cc, z)

    def column(zz):
        return (dp, zz)

    def step(i, k, n):
        return lax.rem(i + k, n)

    partner = plane(y, x, 1 - core)

    def along(half, k):
        return plane(y, step(x, k, NX), core) if half == 0 else plane(step(y, k, NY), x, core)

    barrier = pltpu.get_barrier_semaphore()
    for k in range(1, NZ):
        pl.semaphore_signal(barrier, inc=1, device_id=column(step(z, k, NZ)), device_id_type=MESH)
    pl.semaphore_signal(barrier, inc=1, device_id=partner, device_id_type=MESH)
    for half in range(2):
        for k in range(1, 4):
            pl.semaphore_signal(barrier, inc=1, device_id=along(half, k), device_id_type=MESH)

    def remote(src, dst, send, recv, to):
        return pltpu.make_async_remote_copy(
            src_ref=src, dst_ref=dst, send_sem=send, recv_sem=recv, device_id=to, device_id_type=MESH
        )

    def chunk(half, k, cc):
        if half == 0:
            return p_ref.at[:, step(x, k, NX), cc, pl.ds(0, 4)]
        return p_ref.at[step(y, k, NY), :, cc, pl.ds(4, 4)]

    def to_partner(half, k):
        return remote(asend.at[half, k], arecv.at[half, k], a_send.at[half, k], a_recv.at[half, k], partner)

    def load(half, k, cc, dst, sem):
        return pltpu.make_async_copy(chunk(half, k, cc), dst.at[half, k], sem.at[half, k])

    def load_mine(half, k):
        return load(half, k, core, own, own_sem)

    def load_theirs(half, k):
        return load(half, k, 1 - core, theirs, their_sem)

    def rows(k, source, to, run):
        at = column(step(z, k, NZ))
        whole = lax.rem(source // 8 + to, 2) == 0
        part = pl.ds(pl.multiple_of((source // 8) * H, H), H)

        @pl.when(whole)
        def _():
            run(remote(s_ref.at[to], smat.at[source], s_send.at[k], s_recv.at[k], at))

        @pl.when(jnp.logical_not(whole))
        def _():
            run(remote(s_ref.at[to, :, part], smat.at[source, :, part], s_send.at[k], s_recv.at[k], at))

    def rows_to(k, run):
        rows(k, z, step(z, k, NZ), run)

    def rows_from(k, run):
        rows(k, step(z, NZ - k, NZ), z, run)

    ORDER = (2, 1, 3, 0)

    def halves_of(ref, half, k, first, count):
        at = ref.at[half, k, pl.ds(first, count)]
        return tuple(at[:, :, :, i : i + H].reshape(count * 4, ROWS, H) for i in (0, H))

    def put(ref, half, k, first, count, halves):
        at = ref.at[half, k, pl.ds(first, count)]
        at[:, :, :, :H] = halves[0].reshape(count, 4, ROWS, H)
        at[:, :, :, H:] = halves[1].reshape(count, 4, ROWS, H)

    def plus(*terms):
        return tuple(sum(t[1:], t[0]) for t in zip(*terms))

    for k in ORDER:
        for half in range(2):
            load_theirs(half, k).start()
    for k in ORDER:
        for half in range(2):
            load_mine(half, k).start()
    pl.semaphore_wait(barrier, NZ - 1 + 1 + 6)
    for k in (8, 7, 9, 6, 10, 5, 11, 4, 12, 3, 13, 2, 14, 1, 15):
        rows_to(k, lambda c: c.start())
    for k in ORDER:
        for half in range(2):
            load_theirs(half, k).wait()
            encode(halves_of(theirs, half, k, 0, 4), asend.at[half, k])
            to_partner(half, k).start()
    own_rows = pltpu.make_async_copy(s_ref.at[z], smat.at[z], s_recv.at[0])
    own_rows.start()
    all_rows = pltpu.make_async_copy(s_ref, srows, stat_sem)
    all_rows.start()

    def b_copy(kind, half, d):
        at = (kind, half, d)
        return remote(bsend.at[at], brecv.at[at], b_send.at[at], b_recv.at[at], along(half, 1 + 2 * d))

    def b_start(kind, half, d, halves):
        encode(halves, bsend.at[kind, half, d])
        b_copy(kind, half, d).start()

    def b_get(kind, half, d):
        b_copy(kind, half, d).wait_recv()
        return decode(brecv.at[kind, half, d], 8)

    def c_copy(half, k):
        return remote(csend.at[half, k - 1], crecv.at[half, k - 1], c_send.at[half, k - 1], c_recv.at[half, k - 1], along(1 - half, k))

    for k in ORDER:
        for half in range(2):
            to_partner(half, k).wait_recv()
            load_mine(half, k).wait()
            total = plus(halves_of(own, half, k, 0, 4), decode(arecv.at[half, k], 16))
            low, high = tuple(t[:8] for t in total), tuple(t[8:] for t in total)
            if k == 2:
                b_start(0, half, 0, low)
                b_start(0, half, 1, high)
            elif k == 1:
                b_start(1, half, 0, high)
                put(own, half, 1, 0, 2, low)
            elif k == 3:
                b_start(1, half, 1, low)
                put(own, half, 3, 2, 2, high)
            else:
                put(own, half, 0, 0, 4, total)
    for half in range(2):
        b_start(2, half, 0, plus(halves_of(own, half, 1, 0, 2), b_get(0, half, 0)))
        b_start(2, half, 1, plus(halves_of(own, half, 3, 2, 2), b_get(0, half, 1)))

    right_z, left_z = column(step(z, 1, NZ)), column(step(z, NZ - 1, NZ))

    def ring(buf, parts, right_sem, left_sem, recv):
        def hop(d, s, p):
            origin = step(z, NZ - s, NZ) if d == 0 else step(z, s, NZ)
            at = buf.at[origin, pl.ds(*parts[p])]
            sem = (right_sem if d == 0 else left_sem).at[s, p]
            return remote(at, at, sem, recv.at[origin, p], right_z if d == 0 else left_z)

        def arrive(d, s, p):
            if s < 8 or p == d:
                c = hop(d, s, p)
                c.wait_recv()
                if s < 7 or (s == 7 and p == d):
                    c.start()

        def begin():
            for p in range(2):
                for d in range(2):
                    hop(d, 0, p).start()

        def finish():
            for p in range(2):
                for d in range(2):
                    for s in range(8 if p == d else 7):
                        hop(d, s, p).wait_send()

        return arrive, begin, finish

    g_arrive, g_begin, g_finish = ring(gq, G_PARTS, g_right, g_left, g_recv)
    r_arrive, r_begin, r_finish = ring(rq, R_PARTS, r_right, r_left, r_recv)

    def unpack_g(origin):
        a, b = decode(gq.at[origin], NB)
        ah, al = split(a)
        bh, bl = split(b)
        ghi[origin, :, :, :H] = ah
        ghi[origin, :, :, H:] = bh
        glo[origin, :, :, :H] = al
        glo[origin, :, :, H:] = bl

    def plane_sums():
        for half in range(2):
            put(own, half, 0, 0, 2, plus(halves_of(own, half, 0, 0, 2), b_get(1, half, 1), b_get(2, half, 0)))
            put(own, half, 0, 2, 2, plus(halves_of(own, half, 0, 2, 2), b_get(1, half, 0), b_get(2, half, 1)))
            me = y if half == 0 else x
            for k in (2, 1, 3):
                encode(halves_of(own, half, 0, step(me, k, 4), 1), csend.at[half, k - 1])
                c_copy(half, k).start()

    def own_sums():
        for half in range(2):
            me = y if half == 0 else x
            total = halves_of(own, half, 0, me, 1)
            for k in (1, 3, 2):
                c_copy(half, k).wait_recv()
                total = plus(total, decode(crecv.at[half, k - 1], 4))
            gown[pl.ds(4 * half, 4), :, :H], gown[pl.ds(4 * half, 4), :, H:] = total
        encode((gown[:, :, :H], gown[:, :, H:]), gq.at[z])

    def g_step(s):
        for p in range(2):
            g_arrive(0, s, p)
            g_arrive(1, s, p)

    def unpack_step(s):
        unpack_g(step(z, NZ - s, NZ))
        if s < 8:
            unpack_g(step(z, s, NZ))

    def iteration():
        current = cur[...]
        f = factor_of(current)
        fs, rs = split(f), split(root[...])
        both = tuple(jnp.concatenate([u, v], axis=0) for u, v in zip(fs, rs))
        product = dot3(both, fs)
        root[...] = product[N:]
        cur[...] = powered(fs, product[:N], current)

    plane_sums()

    own_rows.wait()
    for k in range(1, NZ):
        rows_from(k, lambda c: c.wait_recv())

    @pl.when(lax.rem(z, 2) == 0)
    def _():
        smat[8:16, :, :H] = smat[0:8, :, H:].reshape(H, H).T.reshape(8, ROWS, H)

    @pl.when(lax.rem(z, 2) == 1)
    def _():
        smat[0:8, :, H:] = smat[8:16, :, :H].reshape(H, H).T.reshape(8, ROWS, H)

    eye = (lax.broadcasted_iota(I32, (N, N), 0) == lax.broadcasted_iota(I32, (N, N), 1)).astype(F32)

    def factor_of(current):
        return (5.0 * eye - current) * 0.25

    def powered(f, square, current):
        s = split(square)
        q = dot3(s, s)
        return dot3(split(q), split(current))

    matrix = smat[...].reshape(N, N)
    magnitude = jnp.sqrt(jnp.sum(matrix * matrix, keepdims=True) + 1e-6)
    current = matrix / magnitude
    f = factor_of(current)
    root[...] = f * lax.rsqrt(jnp.sqrt(magnitude))
    fs = split(f)
    cur[...] = powered(fs, dot3(fs, fs), current)

    iteration()
    own_sums()
    g_begin()
    iteration()
    iteration()
    g_step(1)
    iteration()
    iteration()
    g_step(2)
    last = dot3(split(root[...]), split(factor_of(cur[...])))
    encode_root(last, rq.at[z])
    r_begin()

    def r_step(s, *units):
        units = units + (None,) * 4
        for i, (p, d) in enumerate(((0, 0), (0, 1), (1, 0), (1, 1))):
            r_arrive(d, s, p)
            if units[i] is not None:
                units[i]()

    unpack_g(z)
    unpack_step(1)
    for s in range(1, 4):
        g_step(2 * s + 1)
        unpack_step(2 * s)
        r_step(s)
        g_step(2 * s + 2)
        unpack_step(2 * s + 1)
    unpack_step(8)
    all_rows.wait()

    pick = (
        lax.broadcasted_iota(I32, (ROWS, N), 1) == lax.broadcasted_iota(I32, (ROWS, N), 0) + z * ROWS
    ).astype(F32).astype(BF16)

    def halves(b):
        return ghi[:, b].reshape(N, N), glo[:, b].reshape(N, N)

    def statistics(b):
        gh, gl = halves(b)
        rh, rl = split(gown[b])
        one = dot_nt(jnp.concatenate([rh, rl, pick], axis=0), gh)
        two = dot_nt(jnp.concatenate([rh, pick], axis=0), gl)
        new_ref[2 * b] = srows[2 * b] + one[:16] + (one[16:32] + two[:16])
        ch, cl = one[32:48].astype(BF16), two[16:32].astype(BF16)
        three = dot(jnp.concatenate([ch, cl], axis=0), gh)
        new_ref[2 * b + 1] = srows[2 * b + 1] + three[:16] + (three[16:32] + dot(ch, gl))

    pick_low = (
        lax.broadcasted_iota(I32, (ROWS, H), 1)
        == lax.broadcasted_iota(I32, (ROWS, H), 0) + (z - 8) * ROWS
    ).astype(F32).astype(BF16)

    def precondition(t):
        b = step(pair, t, NB)
        gh, gl = halves(b)
        q = rq[2 * b]
        down = unit(q[24])
        bh, bl = split((value(q[8:16]) * down[None]).reshape(H, H))
        upper = value(rq[2 * b, lax.rem(z, 8)]) * down
        lower = dot_nt(pick_low, bh) + dot_nt(pick_low, bl)
        rows = jnp.concatenate([jnp.where(z < 8, upper, lower), value(rq[2 * b, 8 + z]) * down], axis=1)
        lh, ll = split(rows)
        shaped = dot(jnp.concatenate([lh, ll], axis=0), gh)
        shaped = shaped[:16] + (shaped[16:] + dot(lh, gl))
        a, c, d = decode_root(rq[2 * b + 1])
        right = jnp.concatenate(
            [jnp.concatenate([a, c], axis=1), jnp.concatenate([c.T, d], axis=1)], axis=0
        )
        rh, rl = split(right)
        sh, sl = split(shaped)
        out = dot(jnp.concatenate([sh, sl], axis=0), rh)
        pre_ref[b] = out[:16] + (out[16:] + dot(sh, rl))

    pair = z // 2

    def stat(b):
        return lambda: statistics(b)

    def pre(t):
        return lambda: precondition(t)

    r_step(4, stat(0), stat(1), pre(0), stat(2))
    r_step(5, stat(3), pre(1), stat(4), pre(7))
    r_step(6, stat(5), pre(2), stat(6), pre(6))
    r_step(7, stat(7))
    r_step(8, pre(3), None, pre(5))
    precondition(4)

    for half in range(2):
        for k in range(4):
            to_partner(half, k).wait_send()
        for kind in range(3):
            for d in range(2):
                b_copy(kind, half, d).wait_send()
        for k in range(1, 4):
            c_copy(half, k).wait_send()
    for k in range(1, NZ):
        rows_to(k, lambda c: c.wait_send())
    g_finish()
    r_finish()


def output_kernel(owner_ref, pre_in, new_in, rq, pre_ref, new_ref, kept_ref, sem):
    dp = lax.axis_index("dp")
    z = lax.axis_index("owner")
    copies = [
        pltpu.make_async_copy(src, dst, sem.at[i])
        for i, (src, dst) in enumerate(((pre_in, pre_ref), (new_in, new_ref)))
    ]
    for copy in copies:
        copy.start()

    first, second, count = jnp.int32(0), jnp.int32(0), jnp.int32(0)
    for j in range(16):
        hit = owner_ref[dp * 16 + j] == z
        first = jnp.where(hit & (count == 0), j, first)
        second = jnp.where(hit & (count == 1), j, second)
        count = count + hit.astype(I32)
    for slot, j in enumerate((first, second)):
        live = (count > slot).astype(F32)
        a, c, d = decode_root(rq[j])
        kept_ref[slot, 0:8, :, :H] = (a * live).astype(BF16).reshape(8, ROWS, H)
        kept_ref[slot, 0:8, :, H:] = (c * live).astype(BF16).reshape(8, ROWS, H)
        kept_ref[slot, 8:16, :, :H] = (c.T * live).astype(BF16).reshape(8, ROWS, H)
        kept_ref[slot, 8:16, :, H:] = (d * live).astype(BF16).reshape(8, ROWS, H)

    for copy in copies:
        copy.wait()


def shards(partials, statistics, assignment):
    vmem, dma = pltpu.VMEM, pltpu.SemaphoreType.DMA
    in_vmem, in_hbm = pl.BlockSpec(memory_space=pltpu.VMEM), pl.BlockSpec(memory_space=pl.ANY)
    shapes = (
        jax.ShapeDtypeStruct((NB, ROWS, N), F32),
        jax.ShapeDtypeStruct((2 * NB, ROWS, N), F32),
    )
    pre, new, rq = pl.pallas_call(
        kernel,
        out_shape=(*shapes, jax.ShapeDtypeStruct((NZ, R_MSG, ROWS, H), I16)),
        in_specs=[in_hbm] * 2,
        out_specs=[in_vmem] * 3,
        scratch_shapes=[
            vmem((2 * NB, ROWS, N), F32),
            vmem((2, 4, 4, 4, ROWS, N), F32),
            vmem((2, 4, 4, 4, ROWS, N), F32),
            vmem((2, 4, A_MSG, ROWS, H), I16),
            vmem((2, 4, A_MSG, ROWS, H), I16),
            vmem((3, 2, 2, B_MSG, ROWS, H), I16),
            vmem((3, 2, 2, B_MSG, ROWS, H), I16),
            vmem((2, 3, C_MSG, ROWS, H), I16),
            vmem((2, 3, C_MSG, ROWS, H), I16),
            vmem((NB, ROWS, N), F32),
            vmem((NZ, ROWS, N), F32),
            vmem((N, N), F32),
            vmem((N, N), F32),
            vmem((NZ, G_MSG, ROWS, H), I16),
            vmem((NZ, NB, ROWS, N), BF16),
            vmem((NZ, NB, ROWS, N), BF16),
            dma((2, 4)), dma((2, 4)), dma, dma((2, 4)), dma((2, 4)),
            dma((3, 2, 2)), dma((3, 2, 2)), dma((2, 3)), dma((2, 3)),
            dma((NZ,)), dma((NZ,)),
            dma((8, 2)), dma((8, 2)), dma((NZ, 2)),
            dma((8, 2)), dma((8, 2)), dma((NZ, 2)),
        ],
        compiler_params=pltpu.CompilerParams(
            collective_id=0, has_side_effects=True, vmem_limit_bytes=50 * 1024 * 1024
        ),
        cost_estimate=pl.CostEstimate(flops=3_000_000_000, bytes_accessed=6_000_000, transcendentals=0),
    )(partials.reshape(NY, NX, 2, NB, ROWS, N), statistics.reshape(2 * NB, ROWS, N))
    pre, new, kept = pl.pallas_call(
        output_kernel,
        out_shape=(*shapes, jax.ShapeDtypeStruct((2, 16, 16, N), BF16)),
        in_specs=[pl.BlockSpec(memory_space=pltpu.SMEM)] + [in_vmem] * 3,
        out_specs=[in_hbm, in_hbm, in_vmem],
        scratch_shapes=[dma((2,))],
        compiler_params=pltpu.CompilerParams(vmem_limit_bytes=32 * 1024 * 1024),
        cost_estimate=pl.CostEstimate(flops=1_000_000, bytes_accessed=1_300_000, transcendentals=0),
    )(assignment.reshape(-1), pre, new, rq)
    return pre, new.reshape(NB, 2, ROWS, N), kept.reshape(1, 1, 2, N, N)


def solution(mesh):
    placed = (P("dp", None, "owner", None), P("dp", None, "owner", None), P())
    return jax.shard_map(
        shards,
        mesh=mesh,
        in_specs=placed,
        out_specs=(
            P("dp", "owner", None),
            P("dp", None, "owner", None),
            P("dp", "owner", None, None, None),
        ),
        check_vma=False,
    )
```

```python
import jax
import jax.numpy as jnp
from jax import lax
from jax.experimental import pallas as pl
from jax.experimental.pallas import tpu as pltpu
from jax.sharding import PartitionSpec as P

MESH = pl.DeviceIdType.MESH
F32, BF16, I16, I32 = jnp.float32, jnp.bfloat16, jnp.int16, jnp.int32
NX = NY = 4
NZ = 16
NB = 8
ROWS = 16
N = 256
H = 128
ITERS = 7
LEVELS = 32760.0 / 32768.0
A_MSG, B_MSG, C_MSG, G_MSG, R_MSG = 33, 17, 9, 17, 25
G_PARTS = ((0, 9), (9, 8))
R_PARTS = ((0, 13), (13, 12))


def code(x):
    return jnp.round(x).astype(I32).astype(I16)


def encode(halves, dst):
    left, right = halves
    m = left.shape[0]
    top = jnp.maximum(jnp.max(jnp.abs(left), axis=0), jnp.max(jnp.abs(right), axis=0))
    e = jnp.ceil(jnp.log2(jnp.maximum(top, 1e-30)))
    up = (jnp.exp2(15.0 - e) * LEVELS)[None]
    dst[0:m] = code(left * up)
    dst[m : 2 * m] = code(right * up)
    dst[2 * m] = code(e)


def value(q):
    return q.astype(I32).astype(F32)


def unit(e):
    return jnp.exp2(value(e) - 15.0) * (1.0 / LEVELS)


def decode(src, m):
    down = unit(src[2 * m])[None]
    return value(src[0:m]) * down, value(src[m : 2 * m]) * down


def encode_root(x, dst):
    x = jnp.concatenate([x[:H, :H], x[:H, H:], x[H:, H:]], axis=0).reshape(24, ROWS, H)
    e = jnp.ceil(jnp.log2(jnp.maximum(jnp.max(jnp.abs(x), axis=0), 1e-30)))
    dst[0:24] = code(x * (jnp.exp2(15.0 - e) * LEVELS)[None])
    dst[24] = code(e)


def decode_root(q):
    v = (value(q[0:24]) * unit(q[24])[None]).reshape(3 * H, H)
    return v[:H], v[H : 2 * H], v[2 * H :]


def split(x):
    high = x.astype(BF16)
    return high, (x - high.astype(F32)).astype(BF16)


def dot(a, b):
    return jnp.dot(a, b, preferred_element_type=F32)


def dot_nt(a, b):
    return lax.dot_general(a, b, (((1,), (1,)), ((), ())), preferred_element_type=F32)


def dot3(a, b):
    (ah, al), (bh, bl) = a, b
    return dot(ah, bh) + (dot(al, bh) + dot(ah, bl))


def kernel(
    p_ref, s_ref, pre_ref, new_ref, rq,
    srows, own, theirs, asend, arecv, bsend, brecv, csend, crecv, gown, smat, cur, root, gq, ghi, glo,
    own_sem, their_sem, stat_sem, a_send, a_recv, b_send, b_recv, c_send, c_recv, s_send, s_recv,
    g_right, g_left, g_recv, r_right, r_left, r_recv,
):
    dp = lax.axis_index("dp")
    z = lax.axis_index("owner")
    core = lax.rem(dp, 2)
    x = lax.rem(dp // 2, NX)
    y = dp // (2 * NX)

    def plane(yy, xx, cc):
        return ((yy * NX + xx) * 2 + cc, z)

    def column(zz):
        return (dp, zz)

    def step(i, k, n):
        return lax.rem(i + k, n)

    partner = plane(y, x, 1 - core)

    def along(half, k):
        return plane(y, step(x, k, NX), core) if half == 0 else plane(step(y, k, NY), x, core)

    barrier = pltpu.get_barrier_semaphore()
    for k in range(1, NZ):
        pl.semaphore_signal(barrier, inc=1, device_id=column(step(z, k, NZ)), device_id_type=MESH)
    pl.semaphore_signal(barrier, inc=1, device_id=partner, device_id_type=MESH)
    for half in range(2):
        for k in range(1, 4):
            pl.semaphore_signal(barrier, inc=1, device_id=along(half, k), device_id_type=MESH)

    def remote(src, dst, send, recv, to):
        return pltpu.make_async_remote_copy(
            src_ref=src, dst_ref=dst, send_sem=send, recv_sem=recv, device_id=to, device_id_type=MESH
        )

    def chunk(half, k, cc):
        if half == 0:
            return p_ref.at[:, step(x, k, NX), cc, pl.ds(0, 4)]
        return p_ref.at[step(y, k, NY), :, cc, pl.ds(4, 4)]

    def to_partner(half, k):
        return remote(asend.at[half, k], arecv.at[half, k], a_send.at[half, k], a_recv.at[half, k], partner)

    def load(half, k, cc, dst, sem):
        return pltpu.make_async_copy(chunk(half, k, cc), dst.at[half, k], sem.at[half, k])

    def load_mine(half, k):
        return load(half, k, core, own, own_sem)

    def load_theirs(half, k):
        return load(half, k, 1 - core, theirs, their_sem)

    def rows(k, source, to, run):
        at = column(step(z, k, NZ))
        whole = lax.rem(source // 8 + to, 2) == 0
        part = pl.ds(pl.multiple_of((source // 8) * H, H), H)

        @pl.when(whole)
        def _():
            run(remote(s_ref.at[to], smat.at[source], s_send.at[k], s_recv.at[k], at))

        @pl.when(jnp.logical_not(whole))
        def _():
            run(remote(s_ref.at[to, :, part], smat.at[source, :, part], s_send.at[k], s_recv.at[k], at))

    def rows_to(k, run):
        rows(k, z, step(z, k, NZ), run)

    def rows_from(k, run):
        rows(k, step(z, NZ - k, NZ), z, run)

    ORDER = (2, 1, 3, 0)

    def halves_of(ref, half, k, first, count):
        at = ref.at[half, k, pl.ds(first, count)]
        return tuple(at[:, :, :, i : i + H].reshape(count * 4, ROWS, H) for i in (0, H))

    def put(ref, half, k, first, count, halves):
        at = ref.at[half, k, pl.ds(first, count)]
        at[:, :, :, :H] = halves[0].reshape(count, 4, ROWS, H)
        at[:, :, :, H:] = halves[1].reshape(count, 4, ROWS, H)

    def plus(*terms):
        return tuple(sum(t[1:], t[0]) for t in zip(*terms))

    for k in ORDER:
        for half in range(2):
            load_theirs(half, k).start()
    for k in ORDER:
        for half in range(2):
            load_mine(half, k).start()
    pl.semaphore_wait(barrier, NZ - 1 + 1 + 6)
    for k in (8, 7, 9, 6, 10, 5, 11, 4, 12, 3, 13, 2, 14, 1, 15):
        rows_to(k, lambda c: c.start())
    for k in ORDER:
        for half in range(2):
            load_theirs(half, k).wait()
            encode(halves_of(theirs, half, k, 0, 4), asend.at[half, k])
            to_partner(half, k).start()
    own_rows = pltpu.make_async_copy(s_ref.at[z], smat.at[z], s_recv.at[0])
    own_rows.start()
    all_rows = pltpu.make_async_copy(s_ref, srows, stat_sem)
    all_rows.start()

    def b_copy(kind, half, d):
        at = (kind, half, d)
        return remote(bsend.at[at], brecv.at[at], b_send.at[at], b_recv.at[at], along(half, 1 + 2 * d))

    def b_start(kind, half, d, halves):
        encode(halves, bsend.at[kind, half, d])
        b_copy(kind, half, d).start()

    def b_get(kind, half, d):
        b_copy(kind, half, d).wait_recv()
        return decode(brecv.at[kind, half, d], 8)

    def c_copy(half, k):
        return remote(csend.at[half, k - 1], crecv.at[half, k - 1], c_send.at[half, k - 1], c_recv.at[half, k - 1], along(1 - half, k))

    for k in ORDER:
        for half in range(2):
            to_partner(half, k).wait_recv()
            load_mine(half, k).wait()
            total = plus(halves_of(own, half, k, 0, 4), decode(arecv.at[half, k], 16))
            low, high = tuple(t[:8] for t in total), tuple(t[8:] for t in total)
            if k == 2:
                b_start(0, half, 0, low)
                b_start(0, half, 1, high)
            elif k == 1:
                b_start(1, half, 0, high)
                put(own, half, 1, 0, 2, low)
            elif k == 3:
                b_start(1, half, 1, low)
                put(own, half, 3, 2, 2, high)
            else:
                put(own, half, 0, 0, 4, total)
    for half in range(2):
        b_start(2, half, 0, plus(halves_of(own, half, 1, 0, 2), b_get(0, half, 0)))
        b_start(2, half, 1, plus(halves_of(own, half, 3, 2, 2), b_get(0, half, 1)))

    right_z, left_z = column(step(z, 1, NZ)), column(step(z, NZ - 1, NZ))

    def ring(buf, parts, right_sem, left_sem, recv):
        def hop(d, s, p):
            origin = step(z, NZ - s, NZ) if d == 0 else step(z, s, NZ)
            at = buf.at[origin, pl.ds(*parts[p])]
            sem = (right_sem if d == 0 else left_sem).at[s, p]
            return remote(at, at, sem, recv.at[origin, p], right_z if d == 0 else left_z)

        def arrive(d, s, p):
            if s < 8 or p == d:
                c = hop(d, s, p)
                c.wait_recv()
                if s < 7 or (s == 7 and p == d):
                    c.start()

        def begin():
            for p in range(2):
                for d in range(2):
                    hop(d, 0, p).start()

        def finish():
            for p in range(2):
                for d in range(2):
                    for s in range(8 if p == d else 7):
                        hop(d, s, p).wait_send()

        return arrive, begin, finish

    g_arrive, g_begin, g_finish = ring(gq, G_PARTS, g_right, g_left, g_recv)
    r_arrive, r_begin, r_finish = ring(rq, R_PARTS, r_right, r_left, r_recv)

    def unpack_g(origin):
        a, b = decode(gq.at[origin], NB)
        ah, al = split(a)
        bh, bl = split(b)
        ghi[origin, :, :, :H] = ah
        ghi[origin, :, :, H:] = bh
        glo[origin, :, :, :H] = al
        glo[origin, :, :, H:] = bl

    def plane_sums():
        for half in range(2):
            put(own, half, 0, 0, 2, plus(halves_of(own, half, 0, 0, 2), b_get(1, half, 1), b_get(2, half, 0)))
            put(own, half, 0, 2, 2, plus(halves_of(own, half, 0, 2, 2), b_get(1, half, 0), b_get(2, half, 1)))
            me = y if half == 0 else x
            for k in (2, 1, 3):
                encode(halves_of(own, half, 0, step(me, k, 4), 1), csend.at[half, k - 1])
                c_copy(half, k).start()

    def own_sums():
        for half in range(2):
            me = y if half == 0 else x
            total = halves_of(own, half, 0, me, 1)
            for k in (1, 3, 2):
                c_copy(half, k).wait_recv()
                total = plus(total, decode(crecv.at[half, k - 1], 4))
            gown[pl.ds(4 * half, 4), :, :H], gown[pl.ds(4 * half, 4), :, H:] = total
        encode((gown[:, :, :H], gown[:, :, H:]), gq.at[z])

    def g_step(s):
        for p in range(2):
            g_arrive(0, s, p)
            g_arrive(1, s, p)

    def unpack_step(s):
        unpack_g(step(z, NZ - s, NZ))
        if s < 8:
            unpack_g(step(z, s, NZ))

    def iteration():
        current = cur[...]
        f = factor_of(current)
        fs, rs = split(f), split(root[...])
        both = tuple(jnp.concatenate([u, v], axis=0) for u, v in zip(fs, rs))
        product = dot3(both, fs)
        root[...] = product[N:]
        cur[...] = powered(fs, product[:N], current)

    own_rows.wait()
    for k in range(1, NZ):
        rows_from(k, lambda c: c.wait_recv())

    @pl.when(lax.rem(z, 2) == 0)
    def _():
        smat[8:16, :, :H] = smat[0:8, :, H:].reshape(H, H).T.reshape(8, ROWS, H)

    @pl.when(lax.rem(z, 2) == 1)
    def _():
        smat[0:8, :, H:] = smat[8:16, :, :H].reshape(H, H).T.reshape(8, ROWS, H)

    eye = (lax.broadcasted_iota(I32, (N, N), 0) == lax.broadcasted_iota(I32, (N, N), 1)).astype(F32)

    def factor_of(current):
        return (5.0 * eye - current) * 0.25

    def powered(f, square, current):
        s = split(square)
        q = dot3(s, s)
        return dot3(split(q), split(current))

    matrix = smat[...].reshape(N, N)
    magnitude = jnp.sqrt(jnp.sum(matrix * matrix, keepdims=True) + 1e-6)
    current = matrix / magnitude
    f = factor_of(current)
    root[...] = f * lax.rsqrt(jnp.sqrt(magnitude))
    fs = split(f)
    cur[...] = powered(fs, dot3(fs, fs), current)

    plane_sums()
    iteration()
    own_sums()
    g_begin()
    iteration()
    iteration()
    g_step(1)
    iteration()
    iteration()
    g_step(2)
    last = dot3(split(root[...]), split(factor_of(cur[...])))
    encode_root(last, rq.at[z])
    r_begin()

    def r_step(s, *units):
        units = units + (None,) * 4
        for i, (p, d) in enumerate(((0, 0), (0, 1), (1, 0), (1, 1))):
            r_arrive(d, s, p)
            if units[i] is not None:
                units[i]()

    unpack_g(z)
    unpack_step(1)
    for s in range(1, 6):
        g_step(s + 2)
        unpack_step(s + 1)
        r_step(s)
    g_step(8)
    unpack_step(7)
    unpack_step(8)
    all_rows.wait()

    pick = (
        lax.broadcasted_iota(I32, (ROWS, N), 1) == lax.broadcasted_iota(I32, (ROWS, N), 0) + z * ROWS
    ).astype(F32).astype(BF16)

    def halves(b):
        return ghi[:, b].reshape(N, N), glo[:, b].reshape(N, N)

    def statistics(b):
        gh, gl = halves(b)
        rh, rl = split(gown[b])
        one = dot_nt(jnp.concatenate([rh, rl, pick], axis=0), gh)
        two = dot_nt(jnp.concatenate([rh, pick], axis=0), gl)
        new_ref[2 * b] = srows[2 * b] + one[:16] + (one[16:32] + two[:16])
        ch, cl = one[32:48].astype(BF16), two[16:32].astype(BF16)
        three = dot(jnp.concatenate([ch, cl], axis=0), gh)
        new_ref[2 * b + 1] = srows[2 * b + 1] + three[:16] + (three[16:32] + dot(ch, gl))

    pick_low = (
        lax.broadcasted_iota(I32, (ROWS, H), 1)
        == lax.broadcasted_iota(I32, (ROWS, H), 0) + (z - 8) * ROWS
    ).astype(F32).astype(BF16)

    def precondition(t):
        b = step(pair, t, NB)
        gh, gl = halves(b)
        q = rq[2 * b]
        down = unit(q[24])
        bh, bl = split((value(q[8:16]) * down[None]).reshape(H, H))
        upper = value(rq[2 * b, lax.rem(z, 8)]) * down
        lower = dot_nt(pick_low, bh) + dot_nt(pick_low, bl)
        rows = jnp.concatenate([jnp.where(z < 8, upper, lower), value(rq[2 * b, 8 + z]) * down], axis=1)
        lh, ll = split(rows)
        shaped = dot(jnp.concatenate([lh, ll], axis=0), gh)
        shaped = shaped[:16] + (shaped[16:] + dot(lh, gl))
        a, c, d = decode_root(rq[2 * b + 1])
        right = jnp.concatenate(
            [jnp.concatenate([a, c], axis=1), jnp.concatenate([c.T, d], axis=1)], axis=0
        )
        rh, rl = split(right)
        sh, sl = split(shaped)
        out = dot(jnp.concatenate([sh, sl], axis=0), rh)
        pre_ref[b] = out[:16] + (out[16:] + dot(sh, rl))

    pair = z // 2

    def stat(b):
        return lambda: statistics(b)

    def pre(t):
        return lambda: precondition(t)

    r_step(6, stat(0), stat(1), stat(2), stat(3))
    r_step(7, stat(4), stat(5), stat(6), stat(7))
    for t in (0, 1, 7, 2, 6, 3, 5):
        precondition(t)
    r_step(8)
    precondition(4)

    for half in range(2):
        for k in range(4):
            to_partner(half, k).wait_send()
        for kind in range(3):
            for d in range(2):
                b_copy(kind, half, d).wait_send()
        for k in range(1, 4):
            c_copy(half, k).wait_send()
    for k in range(1, NZ):
        rows_to(k, lambda c: c.wait_send())
    g_finish()
    r_finish()


def output_kernel(owner_ref, pre_in, new_in, rq, pre_ref, new_ref, kept_ref, sem):
    dp = lax.axis_index("dp")
    z = lax.axis_index("owner")
    copies = [
        pltpu.make_async_copy(src, dst, sem.at[i])
        for i, (src, dst) in enumerate(((pre_in, pre_ref), (new_in, new_ref)))
    ]
    for copy in copies:
        copy.start()

    first, second, count = jnp.int32(0), jnp.int32(0), jnp.int32(0)
    for j in range(16):
        hit = owner_ref[dp * 16 + j] == z
        first = jnp.where(hit & (count == 0), j, first)
        second = jnp.where(hit & (count == 1), j, second)
        count = count + hit.astype(I32)
    for slot, j in enumerate((first, second)):
        live = (count > slot).astype(F32)
        a, c, d = decode_root(rq[j])
        kept_ref[slot, 0:8, :, :H] = (a * live).astype(BF16).reshape(8, ROWS, H)
        kept_ref[slot, 0:8, :, H:] = (c * live).astype(BF16).reshape(8, ROWS, H)
        kept_ref[slot, 8:16, :, :H] = (c.T * live).astype(BF16).reshape(8, ROWS, H)
        kept_ref[slot, 8:16, :, H:] = (d * live).astype(BF16).reshape(8, ROWS, H)

    for copy in copies:
        copy.wait()


def shards(partials, statistics, assignment):
    vmem, dma = pltpu.VMEM, pltpu.SemaphoreType.DMA
    in_vmem, in_hbm = pl.BlockSpec(memory_space=pltpu.VMEM), pl.BlockSpec(memory_space=pl.ANY)
    shapes = (
        jax.ShapeDtypeStruct((NB, ROWS, N), F32),
        jax.ShapeDtypeStruct((2 * NB, ROWS, N), F32),
    )
    pre, new, rq = pl.pallas_call(
        kernel,
        out_shape=(*shapes, jax.ShapeDtypeStruct((NZ, R_MSG, ROWS, H), I16)),
        in_specs=[in_hbm] * 2,
        out_specs=[in_vmem] * 3,
        scratch_shapes=[
            vmem((2 * NB, ROWS, N), F32),
            vmem((2, 4, 4, 4, ROWS, N), F32),
            vmem((2, 4, 4, 4, ROWS, N), F32),
            vmem((2, 4, A_MSG, ROWS, H), I16),
            vmem((2, 4, A_MSG, ROWS, H), I16),
            vmem((3, 2, 2, B_MSG, ROWS, H), I16),
            vmem((3, 2, 2, B_MSG, ROWS, H), I16),
            vmem((2, 3, C_MSG, ROWS, H), I16),
            vmem((2, 3, C_MSG, ROWS, H), I16),
            vmem((NB, ROWS, N), F32),
            vmem((NZ, ROWS, N), F32),
            vmem((N, N), F32),
            vmem((N, N), F32),
            vmem((NZ, G_MSG, ROWS, H), I16),
            vmem((NZ, NB, ROWS, N), BF16),
            vmem((NZ, NB, ROWS, N), BF16),
            dma((2, 4)), dma((2, 4)), dma, dma((2, 4)), dma((2, 4)),
            dma((3, 2, 2)), dma((3, 2, 2)), dma((2, 3)), dma((2, 3)),
            dma((NZ,)), dma((NZ,)),
            dma((8, 2)), dma((8, 2)), dma((NZ, 2)),
            dma((8, 2)), dma((8, 2)), dma((NZ, 2)),
        ],
        compiler_params=pltpu.CompilerParams(
            collective_id=0, has_side_effects=True, vmem_limit_bytes=50 * 1024 * 1024
        ),
        cost_estimate=pl.CostEstimate(flops=3_000_000_000, bytes_accessed=6_000_000, transcendentals=0),
    )(partials.reshape(NY, NX, 2, NB, ROWS, N), statistics.reshape(2 * NB, ROWS, N))
    pre, new, kept = pl.pallas_call(
        output_kernel,
        out_shape=(*shapes, jax.ShapeDtypeStruct((2, 16, 16, N), BF16)),
        in_specs=[pl.BlockSpec(memory_space=pltpu.SMEM)] + [in_vmem] * 3,
        out_specs=[in_hbm, in_hbm, in_vmem],
        scratch_shapes=[dma((2,))],
        compiler_params=pltpu.CompilerParams(vmem_limit_bytes=32 * 1024 * 1024),
        cost_estimate=pl.CostEstimate(flops=1_000_000, bytes_accessed=1_300_000, transcendentals=0),
    )(assignment.reshape(-1), pre, new, rq)
    return pre, new.reshape(NB, 2, ROWS, N), kept.reshape(1, 1, 2, N, N)


def solution(mesh):
    placed = (P("dp", None, "owner", None), P("dp", None, "owner", None), P())
    return jax.shard_map(
        shards,
        mesh=mesh,
        in_specs=placed,
        out_specs=(
            P("dp", "owner", None),
            P("dp", None, "owner", None),
            P("dp", "owner", None, None, None),
        ),
        check_vma=False,
    )
```

```python
import jax
import jax.numpy as jnp
from jax import lax
from jax.experimental import pallas as pl
from jax.experimental.pallas import tpu as pltpu
from jax.sharding import PartitionSpec as P

MESH = pl.DeviceIdType.MESH
F32, BF16, I16, I32 = jnp.float32, jnp.bfloat16, jnp.int16, jnp.int32
NX = NY = 4
NZ = 16
NB = 8
ROWS = 16
N = 256
H = 128
ITERS = 7
LEVELS = 32760.0 / 32768.0
A_MSG, B_MSG, C_MSG, G_MSG, R_MSG = 33, 17, 9, 17, 18
G_PARTS = ((0, 9), (9, 8))
R_PARTS = ((0, 9), (9, 9))


def code(x):
    return jnp.round(x).astype(I32).astype(I16)


def encode(halves, dst):
    left, right = halves
    m = left.shape[0]
    top = jnp.maximum(jnp.max(jnp.abs(left), axis=0), jnp.max(jnp.abs(right), axis=0))
    e = jnp.ceil(jnp.log2(jnp.maximum(top, 1e-30)))
    up = (jnp.exp2(15.0 - e) * LEVELS)[None]
    dst[0:m] = code(left * up)
    dst[m : 2 * m] = code(right * up)
    dst[2 * m] = code(e)


def value(q):
    return q.astype(I32).astype(F32)


def unit(e):
    return jnp.exp2(value(e) - 15.0) * (1.0 / LEVELS)


def decode(src, m):
    down = unit(src[2 * m])[None]
    return value(src[0:m]) * down, value(src[m : 2 * m]) * down


def square_iota():
    return lax.broadcasted_iota(I32, (H, H), 0), lax.broadcasted_iota(I32, (H, H), 1)


def encode_root(x, dst):
    row, col = square_iota()
    last = x[H:, H:]
    folded = jnp.where(row <= col, x[:H, :H], last)
    diagonal = jnp.sum(jnp.where(row == col, last, 0.0), axis=0, keepdims=True)
    diagonal = jnp.where(row[:ROWS] == 0, diagonal, 0.0)
    x = jnp.concatenate([folded, x[:H, H:], diagonal], axis=0).reshape(17, ROWS, H)
    e = jnp.ceil(jnp.log2(jnp.maximum(jnp.max(jnp.abs(x), axis=0), 1e-30)))
    dst[0:17] = code(x * (jnp.exp2(15.0 - e) * LEVELS)[None])
    dst[17] = code(e)


def decode_root(q):
    v = value(q[0:17]) * unit(q[17])[None]
    folded, upper, diagonal = v[0:8].reshape(H, H), v[8:16].reshape(H, H), v[16][0:1]
    row, col = square_iota()
    turned = folded.T
    return (
        jnp.where(row <= col, folded, turned),
        upper,
        jnp.where(row > col, folded, jnp.where(row == col, diagonal, turned)),
    )


def split(x):
    high = x.astype(BF16)
    return high, (x - high.astype(F32)).astype(BF16)


def dot(a, b):
    return jnp.dot(a, b, preferred_element_type=F32)


def dot_nt(a, b):
    return lax.dot_general(a, b, (((1,), (1,)), ((), ())), preferred_element_type=F32)


def dot3(a, b):
    (ah, al), (bh, bl) = a, b
    return dot(ah, bh) + (dot(al, bh) + dot(ah, bl))


def kernel(
    p_ref, s_ref, pre_ref, new_ref, rq,
    srows, own, theirs, asend, arecv, bsend, brecv, csend, crecv, gown, smat, cur, root, gq, ghi, glo,
    own_sem, their_sem, stat_sem, a_send, a_recv, b_send, b_recv, c_send, c_recv, s_send, s_recv,
    g_right, g_left, g_recv, r_right, r_left, r_recv,
):
    dp = lax.axis_index("dp")
    z = lax.axis_index("owner")
    core = lax.rem(dp, 2)
    x = lax.rem(dp // 2, NX)
    y = dp // (2 * NX)

    def plane(yy, xx, cc):
        return ((yy * NX + xx) * 2 + cc, z)

    def column(zz):
        return (dp, zz)

    def step(i, k, n):
        return lax.rem(i + k, n)

    partner = plane(y, x, 1 - core)

    def along(half, k):
        return plane(y, step(x, k, NX), core) if half == 0 else plane(step(y, k, NY), x, core)

    barrier = pltpu.get_barrier_semaphore()
    for k in range(1, NZ):
        pl.semaphore_signal(barrier, inc=1, device_id=column(step(z, k, NZ)), device_id_type=MESH)
    pl.semaphore_signal(barrier, inc=1, device_id=partner, device_id_type=MESH)
    for half in range(2):
        for k in range(1, 4):
            pl.semaphore_signal(barrier, inc=1, device_id=along(half, k), device_id_type=MESH)

    def remote(src, dst, send, recv, to):
        return pltpu.make_async_remote_copy(
            src_ref=src, dst_ref=dst, send_sem=send, recv_sem=recv, device_id=to, device_id_type=MESH
        )

    def chunk(half, k, cc):
        if half == 0:
            return p_ref.at[:, step(x, k, NX), cc, pl.ds(0, 4)]
        return p_ref.at[step(y, k, NY), :, cc, pl.ds(4, 4)]

    def to_partner(half, k):
        return remote(asend.at[half, k], arecv.at[half, k], a_send.at[half, k], a_recv.at[half, k], partner)

    def load(half, k, cc, dst, sem):
        return pltpu.make_async_copy(chunk(half, k, cc), dst.at[half, k], sem.at[half, k])

    def load_mine(half, k):
        return load(half, k, core, own, own_sem)

    def load_theirs(half, k):
        return load(half, k, 1 - core, theirs, their_sem)

    def rows(k, source, to, run):
        at = column(step(z, k, NZ))
        whole = lax.rem(source // 8 + to, 2) == 0
        part = pl.ds(pl.multiple_of((source // 8) * H, H), H)

        @pl.when(whole)
        def _():
            run(remote(s_ref.at[to], smat.at[source], s_send.at[k], s_recv.at[k], at))

        @pl.when(jnp.logical_not(whole))
        def _():
            run(remote(s_ref.at[to, :, part], smat.at[source, :, part], s_send.at[k], s_recv.at[k], at))

    def rows_to(k, run):
        rows(k, z, step(z, k, NZ), run)

    def rows_from(k, run):
        rows(k, step(z, NZ - k, NZ), z, run)

    ORDER = (2, 1, 3, 0)

    def halves_of(ref, half, k, first, count):
        at = ref.at[half, k, pl.ds(first, count)]
        return tuple(at[:, :, :, i : i + H].reshape(count * 4, ROWS, H) for i in (0, H))

    def put(ref, half, k, first, count, halves):
        at = ref.at[half, k, pl.ds(first, count)]
        at[:, :, :, :H] = halves[0].reshape(count, 4, ROWS, H)
        at[:, :, :, H:] = halves[1].reshape(count, 4, ROWS, H)

    def plus(*terms):
        return tuple(sum(t[1:], t[0]) for t in zip(*terms))

    for k in ORDER:
        for half in range(2):
            load_theirs(half, k).start()
    for k in ORDER:
        for half in range(2):
            load_mine(half, k).start()
    pl.semaphore_wait(barrier, NZ - 1 + 1 + 6)
    for k in (8, 7, 9, 6, 10, 5, 11, 4, 12, 3, 13, 2, 14, 1, 15):
        rows_to(k, lambda c: c.start())
    for k in ORDER:
        for half in range(2):
            load_theirs(half, k).wait()
            encode(halves_of(theirs, half, k, 0, 4), asend.at[half, k])
            to_partner(half, k).start()
    own_rows = pltpu.make_async_copy(s_ref.at[z], smat.at[z], s_recv.at[0])
    own_rows.start()
    all_rows = pltpu.make_async_copy(s_ref, srows, stat_sem)
    all_rows.start()

    def b_copy(kind, half, d):
        at = (kind, half, d)
        return remote(bsend.at[at], brecv.at[at], b_send.at[at], b_recv.at[at], along(half, 1 + 2 * d))

    def b_start(kind, half, d, halves):
        encode(halves, bsend.at[kind, half, d])
        b_copy(kind, half, d).start()

    def b_get(kind, half, d):
        b_copy(kind, half, d).wait_recv()
        return decode(brecv.at[kind, half, d], 8)

    def c_copy(half, k):
        return remote(csend.at[half, k - 1], crecv.at[half, k - 1], c_send.at[half, k - 1], c_recv.at[half, k - 1], along(1 - half, k))

    for k in ORDER:
        for half in range(2):
            to_partner(half, k).wait_recv()
            load_mine(half, k).wait()
            total = plus(halves_of(own, half, k, 0, 4), decode(arecv.at[half, k], 16))
            low, high = tuple(t[:8] for t in total), tuple(t[8:] for t in total)
            if k == 2:
                b_start(0, half, 0, low)
                b_start(0, half, 1, high)
            elif k == 1:
                b_start(1, half, 0, high)
                put(own, half, 1, 0, 2, low)
            elif k == 3:
                b_start(1, half, 1, low)
                put(own, half, 3, 2, 2, high)
            else:
                put(own, half, 0, 0, 4, total)
    for half in range(2):
        b_start(2, half, 0, plus(halves_of(own, half, 1, 0, 2), b_get(0, half, 0)))
        b_start(2, half, 1, plus(halves_of(own, half, 3, 2, 2), b_get(0, half, 1)))

    right_z, left_z = column(step(z, 1, NZ)), column(step(z, NZ - 1, NZ))

    def ring(buf, parts, right_sem, left_sem, recv):
        def hop(d, s, p):
            origin = step(z, NZ - s, NZ) if d == 0 else step(z, s, NZ)
            at = buf.at[origin, pl.ds(*parts[p])]
            sem = (right_sem if d == 0 else left_sem).at[s, p]
            return remote(at, at, sem, recv.at[origin, p], right_z if d == 0 else left_z)

        def arrive(d, s, p):
            if s < 8 or p == d:
                c = hop(d, s, p)
                c.wait_recv()
                if s < 7 or (s == 7 and p == d):
                    c.start()

        def begin():
            for p in range(2):
                for d in range(2):
                    hop(d, 0, p).start()

        def finish():
            for p in range(2):
                for d in range(2):
                    for s in range(8 if p == d else 7):
                        hop(d, s, p).wait_send()

        return arrive, begin, finish

    g_arrive, g_begin, g_finish = ring(gq, G_PARTS, g_right, g_left, g_recv)
    r_arrive, r_begin, r_finish = ring(rq, R_PARTS, r_right, r_left, r_recv)

    def unpack_g(origin):
        a, b = decode(gq.at[origin], NB)
        ah, al = split(a)
        bh, bl = split(b)
        ghi[origin, :, :, :H] = ah
        ghi[origin, :, :, H:] = bh
        glo[origin, :, :, :H] = al
        glo[origin, :, :, H:] = bl

    def plane_sums():
        for half in range(2):
            put(own, half, 0, 0, 2, plus(halves_of(own, half, 0, 0, 2), b_get(1, half, 1), b_get(2, half, 0)))
            put(own, half, 0, 2, 2, plus(halves_of(own, half, 0, 2, 2), b_get(1, half, 0), b_get(2, half, 1)))
            me = y if half == 0 else x
            for k in (2, 1, 3):
                encode(halves_of(own, half, 0, step(me, k, 4), 1), csend.at[half, k - 1])
                c_copy(half, k).start()

    def own_sums():
        for half in range(2):
            me = y if half == 0 else x
            total = halves_of(own, half, 0, me, 1)
            for k in (1, 3, 2):
                c_copy(half, k).wait_recv()
                total = plus(total, decode(crecv.at[half, k - 1], 4))
            gown[pl.ds(4 * half, 4), :, :H], gown[pl.ds(4 * half, 4), :, H:] = total
        encode((gown[:, :, :H], gown[:, :, H:]), gq.at[z])

    def g_step(s):
        for p in range(2):
            g_arrive(0, s, p)
            g_arrive(1, s, p)

    def unpack_step(s):
        unpack_g(step(z, NZ - s, NZ))
        if s < 8:
            unpack_g(step(z, s, NZ))

    def iteration():
        current = cur[...]
        f = factor_of(current)
        fs, rs = split(f), split(root[...])
        both = tuple(jnp.concatenate([u, v], axis=0) for u, v in zip(fs, rs))
        product = dot3(both, fs)
        root[...] = product[N:]
        cur[...] = powered(fs, product[:N], current)

    own_rows.wait()
    for k in range(1, NZ):
        rows_from(k, lambda c: c.wait_recv())

    @pl.when(lax.rem(z, 2) == 0)
    def _():
        smat[8:16, :, :H] = smat[0:8, :, H:].reshape(H, H).T.reshape(8, ROWS, H)

    @pl.when(lax.rem(z, 2) == 1)
    def _():
        smat[0:8, :, H:] = smat[8:16, :, :H].reshape(H, H).T.reshape(8, ROWS, H)

    eye = (lax.broadcasted_iota(I32, (N, N), 0) == lax.broadcasted_iota(I32, (N, N), 1)).astype(F32)

    def factor_of(current):
        return (5.0 * eye - current) * 0.25

    def powered(f, square, current):
        s = split(square)
        q = dot3(s, s)
        return dot3(split(q), split(current))

    matrix = smat[...].reshape(N, N)
    magnitude = jnp.sqrt(jnp.sum(matrix * matrix, keepdims=True) + 1e-6)
    current = matrix / magnitude
    f = factor_of(current)
    root[...] = f * lax.rsqrt(jnp.sqrt(magnitude))
    fs = split(f)
    cur[...] = powered(fs, dot3(fs, fs), current)

    plane_sums()
    iteration()
    own_sums()
    g_begin()
    iteration()
    iteration()
    g_step(1)
    iteration()
    iteration()
    g_step(2)
    last = dot3(split(root[...]), split(factor_of(cur[...])))
    encode_root(last, rq.at[z])
    r_begin()

    def r_step(s, *units):
        units = units + (None,) * 4
        for i, (p, d) in enumerate(((0, 0), (0, 1), (1, 0), (1, 1))):
            r_arrive(d, s, p)
            if units[i] is not None:
                units[i]()

    unpack_g(z)
    unpack_step(1)
    for s in range(1, 6):
        g_step(s + 2)
        unpack_step(s + 1)
        r_step(s)
    g_step(8)
    unpack_step(7)
    unpack_step(8)
    all_rows.wait()

    pick = (
        lax.broadcasted_iota(I32, (ROWS, N), 1) == lax.broadcasted_iota(I32, (ROWS, N), 0) + z * ROWS
    ).astype(F32).astype(BF16)

    def halves(b):
        return ghi[:, b].reshape(N, N), glo[:, b].reshape(N, N)

    def statistics(b):
        gh, gl = halves(b)
        rh, rl = split(gown[b])
        one = dot_nt(jnp.concatenate([rh, rl, pick], axis=0), gh)
        two = dot_nt(jnp.concatenate([rh, pick], axis=0), gl)
        new_ref[2 * b] = srows[2 * b] + one[:16] + (one[16:32] + two[:16])
        ch, cl = one[32:48].astype(BF16), two[16:32].astype(BF16)
        three = dot(jnp.concatenate([ch, cl], axis=0), gh)
        new_ref[2 * b + 1] = srows[2 * b + 1] + three[:16] + (three[16:32] + dot(ch, gl))

    z8 = lax.rem(z, 8)
    line = lax.broadcasted_iota(I32, (ROWS, H), 0) + z8 * ROWS
    lane = lax.broadcasted_iota(I32, (ROWS, H), 1)
    pick_in = (lane == line).astype(F32).astype(BF16)

    def precondition(t):
        b = step(pair, t, NB)
        gh, gl = halves(b)
        q = rq[2 * b]
        down = unit(q[17])
        high, low = split((value(q[0:16]) * down[None]).reshape(2 * H, H))
        turned = dot_nt(pick_in, high) + dot_nt(pick_in, low)
        folded = value(rq[2 * b, z8]) * down
        upper = value(rq[2 * b, 8 + z8]) * down
        diagonal = (value(q[16]) * down)[0:1]
        first = jnp.concatenate([jnp.where(line <= lane, folded, turned[:, :H]), upper], axis=1)
        second = jnp.where(line > lane, folded, jnp.where(line == lane, diagonal, turned[:, :H]))
        rows = jnp.where(z < 8, first, jnp.concatenate([turned[:, H:], second], axis=1))
        lh, ll = split(rows)
        shaped = dot(jnp.concatenate([lh, ll], axis=0), gh)
        shaped = shaped[:16] + (shaped[16:] + dot(lh, gl))
        a, c, d = decode_root(rq[2 * b + 1])
        right = jnp.concatenate(
            [jnp.concatenate([a, c], axis=1), jnp.concatenate([c.T, d], axis=1)], axis=0
        )
        rh, rl = split(right)
        sh, sl = split(shaped)
        out = dot(jnp.concatenate([sh, sl], axis=0), rh)
        pre_ref[b] = out[:16] + (out[16:] + dot(sh, rl))

    pair = z // 2

    def stat(b):
        return lambda: statistics(b)

    def pre(t):
        return lambda: precondition(t)

    r_step(6, stat(0), stat(1), stat(2), stat(3))
    r_step(7, stat(4), stat(5), stat(6), stat(7))
    for t in (0, 1, 7, 2, 6, 3, 5):
        precondition(t)
    r_step(8)
    precondition(4)

    for half in range(2):
        for k in range(4):
            to_partner(half, k).wait_send()
        for kind in range(3):
            for d in range(2):
                b_copy(kind, half, d).wait_send()
        for k in range(1, 4):
            c_copy(half, k).wait_send()
    for k in range(1, NZ):
        rows_to(k, lambda c: c.wait_send())
    g_finish()
    r_finish()


def output_kernel(owner_ref, pre_in, new_in, rq, pre_ref, new_ref, kept_ref, sem):
    dp = lax.axis_index("dp")
    z = lax.axis_index("owner")
    copies = [
        pltpu.make_async_copy(src, dst, sem.at[i])
        for i, (src, dst) in enumerate(((pre_in, pre_ref), (new_in, new_ref)))
    ]
    for copy in copies:
        copy.start()

    first, second, count = jnp.int32(0), jnp.int32(0), jnp.int32(0)
    for j in range(16):
        hit = owner_ref[dp * 16 + j] == z
        first = jnp.where(hit & (count == 0), j, first)
        second = jnp.where(hit & (count == 1), j, second)
        count = count + hit.astype(I32)
    for slot, j in enumerate((first, second)):
        live = (count > slot).astype(F32)
        a, c, d = decode_root(rq[j])
        kept_ref[slot, 0:8, :, :H] = (a * live).astype(BF16).reshape(8, ROWS, H)
        kept_ref[slot, 0:8, :, H:] = (c * live).astype(BF16).reshape(8, ROWS, H)
        kept_ref[slot, 8:16, :, :H] = (c.T * live).astype(BF16).reshape(8, ROWS, H)
        kept_ref[slot, 8:16, :, H:] = (d * live).astype(BF16).reshape(8, ROWS, H)

    for copy in copies:
        copy.wait()


def shards(partials, statistics, assignment):
    vmem, dma = pltpu.VMEM, pltpu.SemaphoreType.DMA
    in_vmem, in_hbm = pl.BlockSpec(memory_space=pltpu.VMEM), pl.BlockSpec(memory_space=pl.ANY)
    shapes = (
        jax.ShapeDtypeStruct((NB, ROWS, N), F32),
        jax.ShapeDtypeStruct((2 * NB, ROWS, N), F32),
    )
    pre, new, rq = pl.pallas_call(
        kernel,
        out_shape=(*shapes, jax.ShapeDtypeStruct((NZ, R_MSG, ROWS, H), I16)),
        in_specs=[in_hbm] * 2,
        out_specs=[in_vmem] * 3,
        scratch_shapes=[
            vmem((2 * NB, ROWS, N), F32),
            vmem((2, 4, 4, 4, ROWS, N), F32),
            vmem((2, 4, 4, 4, ROWS, N), F32),
            vmem((2, 4, A_MSG, ROWS, H), I16),
            vmem((2, 4, A_MSG, ROWS, H), I16),
            vmem((3, 2, 2, B_MSG, ROWS, H), I16),
            vmem((3, 2, 2, B_MSG, ROWS, H), I16),
            vmem((2, 3, C_MSG, ROWS, H), I16),
            vmem((2, 3, C_MSG, ROWS, H), I16),
            vmem((NB, ROWS, N), F32),
            vmem((NZ, ROWS, N), F32),
            vmem((N, N), F32),
            vmem((N, N), F32),
            vmem((NZ, G_MSG, ROWS, H), I16),
            vmem((NZ, NB, ROWS, N), BF16),
            vmem((NZ, NB, ROWS, N), BF16),
            dma((2, 4)), dma((2, 4)), dma, dma((2, 4)), dma((2, 4)),
            dma((3, 2, 2)), dma((3, 2, 2)), dma((2, 3)), dma((2, 3)),
            dma((NZ,)), dma((NZ,)),
            dma((8, 2)), dma((8, 2)), dma((NZ, 2)),
            dma((8, 2)), dma((8, 2)), dma((NZ, 2)),
        ],
        compiler_params=pltpu.CompilerParams(
            collective_id=0, has_side_effects=True, vmem_limit_bytes=50 * 1024 * 1024
        ),
        cost_estimate=pl.CostEstimate(flops=3_000_000_000, bytes_accessed=6_000_000, transcendentals=0),
    )(partials.reshape(NY, NX, 2, NB, ROWS, N), statistics.reshape(2 * NB, ROWS, N))
    pre, new, kept = pl.pallas_call(
        output_kernel,
        out_shape=(*shapes, jax.ShapeDtypeStruct((2, 16, 16, N), BF16)),
        in_specs=[pl.BlockSpec(memory_space=pltpu.SMEM)] + [in_vmem] * 3,
        out_specs=[in_hbm, in_hbm, in_vmem],
        scratch_shapes=[dma((2,))],
        compiler_params=pltpu.CompilerParams(vmem_limit_bytes=32 * 1024 * 1024),
        cost_estimate=pl.CostEstimate(flops=1_000_000, bytes_accessed=1_300_000, transcendentals=0),
    )(assignment.reshape(-1), pre, new, rq)
    return pre, new.reshape(NB, 2, ROWS, N), kept.reshape(1, 1, 2, N, N)


def solution(mesh):
    placed = (P("dp", None, "owner", None), P("dp", None, "owner", None), P())
    return jax.shard_map(
        shards,
        mesh=mesh,
        in_specs=placed,
        out_specs=(
            P("dp", "owner", None),
            P("dp", None, "owner", None),
            P("dp", "owner", None, None, None),
        ),
        check_vma=False,
    )
```

```python
import jax
import jax.numpy as jnp
from jax import lax
from jax.experimental import pallas as pl
from jax.experimental.pallas import tpu as pltpu
from jax.sharding import PartitionSpec as P

MESH = pl.DeviceIdType.MESH
F32, BF16, I16, I32 = jnp.float32, jnp.bfloat16, jnp.int16, jnp.int32
NX = NY = 4
NZ = 16
NB = 8
ROWS = 16
N = 256
H = 128
ITERS = 7
LEVELS = 32760.0 / 32768.0
B_MSG, C_MSG, G_MSG, R_MSG = 17, 9, 17, 18
G_PARTS = ((0, 9), (9, 8))
R_PARTS = ((0, 9), (9, 9))


def code(x):
    return jnp.round(x).astype(I32).astype(I16)


def encode(halves, dst):
    left, right = halves
    m = left.shape[0]
    top = jnp.maximum(jnp.max(jnp.abs(left), axis=0), jnp.max(jnp.abs(right), axis=0))
    e = jnp.ceil(jnp.log2(jnp.maximum(top, 1e-30)))
    up = (jnp.exp2(15.0 - e) * LEVELS)[None]
    dst[0:m] = code(left * up)
    dst[m : 2 * m] = code(right * up)
    dst[2 * m] = code(e)


def value(q):
    return q.astype(I32).astype(F32)


def unit(e):
    return jnp.exp2(value(e) - 15.0) * (1.0 / LEVELS)


def decode(src, m):
    down = unit(src[2 * m])[None]
    return value(src[0:m]) * down, value(src[m : 2 * m]) * down


def square_iota():
    return lax.broadcasted_iota(I32, (H, H), 0), lax.broadcasted_iota(I32, (H, H), 1)


def encode_root(x, dst):
    row, col = square_iota()
    last = x[H:, H:]
    folded = jnp.where(row <= col, x[:H, :H], last)
    diagonal = jnp.sum(jnp.where(row == col, last, 0.0), axis=0, keepdims=True)
    diagonal = jnp.where(row[:ROWS] == 0, diagonal, 0.0)
    x = jnp.concatenate([folded, x[:H, H:], diagonal], axis=0).reshape(17, ROWS, H)
    e = jnp.ceil(jnp.log2(jnp.maximum(jnp.max(jnp.abs(x), axis=0), 1e-30)))
    dst[0:17] = code(x * (jnp.exp2(15.0 - e) * LEVELS)[None])
    dst[17] = code(e)


def decode_root(q):
    v = value(q[0:17]) * unit(q[17])[None]
    folded, upper, diagonal = v[0:8].reshape(H, H), v[8:16].reshape(H, H), v[16][0:1]
    row, col = square_iota()
    turned = folded.T
    return (
        jnp.where(row <= col, folded, turned),
        upper,
        jnp.where(row > col, folded, jnp.where(row == col, diagonal, turned)),
    )


def split(x):
    high = x.astype(BF16)
    return high, (x - high.astype(F32)).astype(BF16)


def dot(a, b):
    return jnp.dot(a, b, preferred_element_type=F32)


def dot_nt(a, b):
    return lax.dot_general(a, b, (((1,), (1,)), ((), ())), preferred_element_type=F32)


def dot3(a, b):
    (ah, al), (bh, bl) = a, b
    return dot(ah, bh) + (dot(al, bh) + dot(ah, bl))


def kernel(
    p_ref, s_ref, pre_ref, new_ref, rq,
    srows, own, theirs, other, bsend, brecv, csend, crecv, gown, smat, cur, root, gq, ghi, glo,
    own_sem, their_sem, stat_sem, a_send, a_recv, b_send, b_recv, c_send, c_recv, s_send, s_recv,
    g_right, g_left, g_recv, r_right, r_left, r_recv,
):
    dp = lax.axis_index("dp")
    z = lax.axis_index("owner")
    core = lax.rem(dp, 2)
    x = lax.rem(dp // 2, NX)
    y = dp // (2 * NX)

    def plane(yy, xx, cc):
        return ((yy * NX + xx) * 2 + cc, z)

    def column(zz):
        return (dp, zz)

    def step(i, k, n):
        return lax.rem(i + k, n)

    partner = plane(y, x, 1 - core)

    def along(half, k):
        return plane(y, step(x, k, NX), core) if half == 0 else plane(step(y, k, NY), x, core)

    barrier = pltpu.get_barrier_semaphore()
    for k in range(1, NZ):
        pl.semaphore_signal(barrier, inc=1, device_id=column(step(z, k, NZ)), device_id_type=MESH)
    pl.semaphore_signal(barrier, inc=1, device_id=partner, device_id_type=MESH)
    for half in range(2):
        for k in range(1, 4):
            pl.semaphore_signal(barrier, inc=1, device_id=along(half, k), device_id_type=MESH)

    def remote(src, dst, send, recv, to):
        return pltpu.make_async_remote_copy(
            src_ref=src, dst_ref=dst, send_sem=send, recv_sem=recv, device_id=to, device_id_type=MESH
        )

    def chunk(half, k, cc):
        if half == 0:
            return p_ref.at[:, step(x, k, NX), cc, pl.ds(0, 4)]
        return p_ref.at[step(y, k, NY), :, cc, pl.ds(4, 4)]

    def to_partner(half, k):
        return remote(theirs.at[half, k], other.at[half, k], a_send.at[half, k], a_recv.at[half, k], partner)

    def load(half, k, cc, dst, sem):
        return pltpu.make_async_copy(chunk(half, k, cc), dst.at[half, k], sem.at[half, k])

    def load_mine(half, k):
        return load(half, k, core, own, own_sem)

    def load_theirs(half, k):
        return load(half, k, 1 - core, theirs, their_sem)

    def rows(k, source, to, run):
        at = column(step(z, k, NZ))
        whole = lax.rem(source // 8 + to, 2) == 0
        part = pl.ds(pl.multiple_of((source // 8) * H, H), H)

        @pl.when(whole)
        def _():
            run(remote(s_ref.at[to], smat.at[source], s_send.at[k], s_recv.at[k], at))

        @pl.when(jnp.logical_not(whole))
        def _():
            run(remote(s_ref.at[to, :, part], smat.at[source, :, part], s_send.at[k], s_recv.at[k], at))

    def rows_to(k, run):
        rows(k, z, step(z, k, NZ), run)

    def rows_from(k, run):
        rows(k, step(z, NZ - k, NZ), z, run)

    ORDER = (2, 1, 3, 0)

    def halves_of(ref, half, k, first, count):
        at = ref.at[half, k, pl.ds(first, count)]
        return tuple(at[:, :, :, i : i + H].reshape(count * 4, ROWS, H) for i in (0, H))

    def put(ref, half, k, first, count, halves):
        at = ref.at[half, k, pl.ds(first, count)]
        at[:, :, :, :H] = halves[0].reshape(count, 4, ROWS, H)
        at[:, :, :, H:] = halves[1].reshape(count, 4, ROWS, H)

    def plus(*terms):
        return tuple(sum(t[1:], t[0]) for t in zip(*terms))

    for k in ORDER:
        for half in range(2):
            load_theirs(half, k).start()
    for k in ORDER:
        for half in range(2):
            load_mine(half, k).start()
    pl.semaphore_wait(barrier, NZ - 1 + 1 + 6)
    def send_share(k):
        for half in range(2):
            load_theirs(half, k).wait()
            to_partner(half, k).start()

    send_share(2)
    for k in (8, 7, 9, 6, 10, 5, 11, 4, 12, 3, 13, 2, 14, 1, 15):
        rows_to(k, lambda c: c.start())
    for k in ORDER[1:]:
        send_share(k)
    own_rows = pltpu.make_async_copy(s_ref.at[z], smat.at[z], s_recv.at[0])
    own_rows.start()
    all_rows = pltpu.make_async_copy(s_ref, srows, stat_sem)
    all_rows.start()

    def b_copy(kind, half, d):
        at = (kind, half, d)
        return remote(bsend.at[at], brecv.at[at], b_send.at[at], b_recv.at[at], along(half, 1 + 2 * d))

    def b_start(kind, half, d, halves):
        encode(halves, bsend.at[kind, half, d])
        b_copy(kind, half, d).start()

    def b_get(kind, half, d):
        b_copy(kind, half, d).wait_recv()
        return decode(brecv.at[kind, half, d], 8)

    def c_copy(half, k):
        return remote(csend.at[half, k - 1], crecv.at[half, k - 1], c_send.at[half, k - 1], c_recv.at[half, k - 1], along(1 - half, k))

    for k in ORDER:
        for half in range(2):
            to_partner(half, k).wait_recv()
            load_mine(half, k).wait()
            total = plus(halves_of(own, half, k, 0, 4), halves_of(other, half, k, 0, 4))
            low, high = tuple(t[:8] for t in total), tuple(t[8:] for t in total)
            if k == 2:
                b_start(0, half, 0, low)
                b_start(0, half, 1, high)
            elif k == 1:
                b_start(1, half, 0, high)
                put(own, half, 1, 0, 2, low)
            elif k == 3:
                b_start(1, half, 1, low)
                put(own, half, 3, 2, 2, high)
            else:
                put(own, half, 0, 0, 4, total)
    for half in range(2):
        b_start(2, half, 0, plus(halves_of(own, half, 1, 0, 2), b_get(0, half, 0)))
        b_start(2, half, 1, plus(halves_of(own, half, 3, 2, 2), b_get(0, half, 1)))

    right_z, left_z = column(step(z, 1, NZ)), column(step(z, NZ - 1, NZ))

    def ring(buf, parts, right_sem, left_sem, recv):
        def hop(d, s, p):
            origin = step(z, NZ - s, NZ) if d == 0 else step(z, s, NZ)
            at = buf.at[origin, pl.ds(*parts[p])]
            sem = (right_sem if d == 0 else left_sem).at[s, p]
            return remote(at, at, sem, recv.at[origin, p], right_z if d == 0 else left_z)

        def arrive(d, s, p):
            if s < 8 or p == d:
                c = hop(d, s, p)
                c.wait_recv()
                if s < 7 or (s == 7 and p == d):
                    c.start()

        def begin():
            for p in range(2):
                for d in range(2):
                    hop(d, 0, p).start()

        def finish(steps):
            for s in steps:
                for p in range(2):
                    for d in range(2):
                        if s < 7 or p == d:
                            hop(d, s, p).wait_send()

        return arrive, begin, finish

    g_arrive, g_begin, g_finish = ring(gq, G_PARTS, g_right, g_left, g_recv)
    r_arrive, r_begin, r_finish = ring(rq, R_PARTS, r_right, r_left, r_recv)

    def unpack_g(origin):
        a, b = decode(gq.at[origin], NB)
        ah, al = split(a)
        bh, bl = split(b)
        ghi[origin, :, :, :H] = ah
        ghi[origin, :, :, H:] = bh
        glo[origin, :, :, :H] = al
        glo[origin, :, :, H:] = bl

    def plane_sums():
        for half in range(2):
            put(own, half, 0, 0, 2, plus(halves_of(own, half, 0, 0, 2), b_get(1, half, 1), b_get(2, half, 0)))
            put(own, half, 0, 2, 2, plus(halves_of(own, half, 0, 2, 2), b_get(1, half, 0), b_get(2, half, 1)))
            me = y if half == 0 else x
            for k in (2, 1, 3):
                encode(halves_of(own, half, 0, step(me, k, 4), 1), csend.at[half, k - 1])
                c_copy(half, k).start()

    def own_sums():
        for half in range(2):
            me = y if half == 0 else x
            total = halves_of(own, half, 0, me, 1)
            for k in (1, 3, 2):
                c_copy(half, k).wait_recv()
                total = plus(total, decode(crecv.at[half, k - 1], 4))
            gown[pl.ds(4 * half, 4), :, :H], gown[pl.ds(4 * half, 4), :, H:] = total
        encode((gown[:, :, :H], gown[:, :, H:]), gq.at[z])

    def g_step(s):
        for p in range(2):
            g_arrive(0, s, p)
            g_arrive(1, s, p)

    def unpack_step(s):
        unpack_g(step(z, NZ - s, NZ))
        if s < 8:
            unpack_g(step(z, s, NZ))

    def iteration():
        current = cur[...]
        f = factor_of(current)
        fs, rs = split(f), split(root[...])
        both = tuple(jnp.concatenate([u, v], axis=0) for u, v in zip(fs, rs))
        product = dot3(both, fs)
        root[...] = product[N:]
        cur[...] = powered(fs, product[:N], current)

    own_rows.wait()
    for k in range(1, NZ):
        rows_from(k, lambda c: c.wait_recv())

    @pl.when(lax.rem(z, 2) == 0)
    def _():
        smat[8:16, :, :H] = smat[0:8, :, H:].reshape(H, H).T.reshape(8, ROWS, H)

    @pl.when(lax.rem(z, 2) == 1)
    def _():
        smat[0:8, :, H:] = smat[8:16, :, :H].reshape(H, H).T.reshape(8, ROWS, H)

    eye = (lax.broadcasted_iota(I32, (N, N), 0) == lax.broadcasted_iota(I32, (N, N), 1)).astype(F32)

    def factor_of(current):
        return (5.0 * eye - current) * 0.25

    def powered(f, square, current):
        s = split(square)
        q = dot3(s, s)
        return dot3(split(q), split(current))

    matrix = smat[...].reshape(N, N)
    magnitude = jnp.sqrt(jnp.sum(matrix * matrix, keepdims=True) + 1e-6)
    current = matrix / magnitude
    f = factor_of(current)
    root[...] = f * lax.rsqrt(jnp.sqrt(magnitude))
    fs = split(f)
    cur[...] = powered(fs, dot3(fs, fs), current)

    plane_sums()
    iteration()
    own_sums()
    g_begin()
    iteration()
    iteration()
    g_step(1)
    iteration()
    iteration()
    g_step(2)
    last = dot3(split(root[...]), split(factor_of(cur[...])))
    encode_root(last, rq.at[z])
    r_begin()

    def r_step(s, *units):
        units = units + (None,) * 4
        for i, (p, d) in enumerate(((0, 0), (0, 1), (1, 0), (1, 1))):
            r_arrive(d, s, p)
            if units[i] is not None:
                units[i]()

    def early_sends():
        for half in range(2):
            for k in range(4):
                to_partner(half, k).wait_send()
            for kind in range(3):
                for d in range(2):
                    b_copy(kind, half, d).wait_send()
            for k in range(1, 4):
                c_copy(half, k).wait_send()
        for k in range(1, NZ):
            rows_to(k, lambda c: c.wait_send())

    unpack_g(z)
    unpack_step(1)
    for s in range(1, 6):
        g_step(s + 2)
        unpack_step(s + 1)
        r_step(s)
        if s == 2:
            early_sends()
    g_step(8)
    unpack_step(7)
    unpack_step(8)
    all_rows.wait()

    pick = (
        lax.broadcasted_iota(I32, (ROWS, N), 1) == lax.broadcasted_iota(I32, (ROWS, N), 0) + z * ROWS
    ).astype(F32).astype(BF16)

    def halves(b):
        return ghi[:, b].reshape(N, N), glo[:, b].reshape(N, N)

    def statistics(b):
        gh, gl = halves(b)
        rh, rl = split(gown[b])
        one = dot_nt(jnp.concatenate([rh, rl, pick], axis=0), gh)
        two = dot_nt(jnp.concatenate([rh, pick], axis=0), gl)
        new_ref[2 * b] = srows[2 * b] + one[:16] + (one[16:32] + two[:16])
        ch, cl = one[32:48].astype(BF16), two[16:32].astype(BF16)
        three = dot(jnp.concatenate([ch, cl], axis=0), gh)
        new_ref[2 * b + 1] = srows[2 * b + 1] + three[:16] + (three[16:32] + dot(ch, gl))

    z8 = lax.rem(z, 8)
    line = lax.broadcasted_iota(I32, (ROWS, H), 0) + z8 * ROWS
    lane = lax.broadcasted_iota(I32, (ROWS, H), 1)
    pick_in = (lane == line).astype(F32).astype(BF16)

    def precondition(t):
        b = step(pair, t, NB)
        gh, gl = halves(b)
        q = rq[2 * b]
        down = unit(q[17])
        high, low = split((value(q[0:16]) * down[None]).reshape(2 * H, H))
        turned = dot_nt(pick_in, high) + dot_nt(pick_in, low)
        folded = value(rq[2 * b, z8]) * down
        upper = value(rq[2 * b, 8 + z8]) * down
        diagonal = (value(q[16]) * down)[0:1]
        first = jnp.concatenate([jnp.where(line <= lane, folded, turned[:, :H]), upper], axis=1)
        second = jnp.where(line > lane, folded, jnp.where(line == lane, diagonal, turned[:, :H]))
        rows = jnp.where(z < 8, first, jnp.concatenate([turned[:, H:], second], axis=1))
        lh, ll = split(rows)
        shaped = dot(jnp.concatenate([lh, ll], axis=0), gh)
        shaped = shaped[:16] + (shaped[16:] + dot(lh, gl))
        a, c, d = decode_root(rq[2 * b + 1])
        right = jnp.concatenate(
            [jnp.concatenate([a, c], axis=1), jnp.concatenate([c.T, d], axis=1)], axis=0
        )
        rh, rl = split(right)
        sh, sl = split(shaped)
        out = dot(jnp.concatenate([sh, sl], axis=0), rh)
        pre_ref[b] = out[:16] + (out[16:] + dot(sh, rl))

    pair = z // 2

    def stat(b):
        return lambda: statistics(b)

    def pre(t):
        return lambda: precondition(t)

    r_step(6, stat(0), stat(1), stat(2), stat(3))
    r_step(7, stat(4), stat(5), stat(6), stat(7))
    for t in (0, 1, 7, 2, 6, 3, 5):
        precondition(t)
    g_finish(range(8))
    r_finish(range(6))
    r_step(8)
    precondition(4)
    r_finish((6, 7))


def output_kernel(owner_ref, pre_in, new_in, rq, pre_ref, new_ref, kept_ref, sem):
    dp = lax.axis_index("dp")
    z = lax.axis_index("owner")
    copies = [
        pltpu.make_async_copy(src, dst, sem.at[i])
        for i, (src, dst) in enumerate(((pre_in, pre_ref), (new_in, new_ref)))
    ]
    for copy in copies:
        copy.start()

    first, second, count = jnp.int32(0), jnp.int32(0), jnp.int32(0)
    for j in range(16):
        hit = owner_ref[dp * 16 + j] == z
        first = jnp.where(hit & (count == 0), j, first)
        second = jnp.where(hit & (count == 1), j, second)
        count = count + hit.astype(I32)
    for slot, j in enumerate((first, second)):
        live = (count > slot).astype(F32)
        a, c, d = decode_root(rq[j])
        kept_ref[slot, 0:8, :, :H] = (a * live).astype(BF16).reshape(8, ROWS, H)
        kept_ref[slot, 0:8, :, H:] = (c * live).astype(BF16).reshape(8, ROWS, H)
        kept_ref[slot, 8:16, :, :H] = (c.T * live).astype(BF16).reshape(8, ROWS, H)
        kept_ref[slot, 8:16, :, H:] = (d * live).astype(BF16).reshape(8, ROWS, H)

    for copy in copies:
        copy.wait()


def shards(partials, statistics, assignment):
    vmem, dma = pltpu.VMEM, pltpu.SemaphoreType.DMA
    in_vmem, in_hbm = pl.BlockSpec(memory_space=pltpu.VMEM), pl.BlockSpec(memory_space=pl.ANY)
    shapes = (
        jax.ShapeDtypeStruct((NB, ROWS, N), F32),
        jax.ShapeDtypeStruct((2 * NB, ROWS, N), F32),
    )
    pre, new, rq = pl.pallas_call(
        kernel,
        out_shape=(*shapes, jax.ShapeDtypeStruct((NZ, R_MSG, ROWS, H), I16)),
        in_specs=[in_hbm] * 2,
        out_specs=[in_vmem] * 3,
        scratch_shapes=[
            vmem((2 * NB, ROWS, N), F32),
            vmem((2, 4, 4, 4, ROWS, N), F32),
            vmem((2, 4, 4, 4, ROWS, N), F32),
            vmem((2, 4, 4, 4, ROWS, N), F32),
            vmem((3, 2, 2, B_MSG, ROWS, H), I16),
            vmem((3, 2, 2, B_MSG, ROWS, H), I16),
            vmem((2, 3, C_MSG, ROWS, H), I16),
            vmem((2, 3, C_MSG, ROWS, H), I16),
            vmem((NB, ROWS, N), F32),
            vmem((NZ, ROWS, N), F32),
            vmem((N, N), F32),
            vmem((N, N), F32),
            vmem((NZ, G_MSG, ROWS, H), I16),
            vmem((NZ, NB, ROWS, N), BF16),
            vmem((NZ, NB, ROWS, N), BF16),
            dma((2, 4)), dma((2, 4)), dma, dma((2, 4)), dma((2, 4)),
            dma((3, 2, 2)), dma((3, 2, 2)), dma((2, 3)), dma((2, 3)),
            dma((NZ,)), dma((NZ,)),
            dma((8, 2)), dma((8, 2)), dma((NZ, 2)),
            dma((8, 2)), dma((8, 2)), dma((NZ, 2)),
        ],
        compiler_params=pltpu.CompilerParams(
            collective_id=0, has_side_effects=True, vmem_limit_bytes=50 * 1024 * 1024
        ),
        cost_estimate=pl.CostEstimate(flops=3_000_000_000, bytes_accessed=6_000_000, transcendentals=0),
    )(partials.reshape(NY, NX, 2, NB, ROWS, N), statistics.reshape(2 * NB, ROWS, N))
    pre, new, kept = pl.pallas_call(
        output_kernel,
        out_shape=(*shapes, jax.ShapeDtypeStruct((2, 16, 16, N), BF16)),
        in_specs=[pl.BlockSpec(memory_space=pltpu.SMEM)] + [in_vmem] * 3,
        out_specs=[in_hbm, in_hbm, in_vmem],
        scratch_shapes=[dma((2,))],
        compiler_params=pltpu.CompilerParams(vmem_limit_bytes=32 * 1024 * 1024),
        cost_estimate=pl.CostEstimate(flops=1_000_000, bytes_accessed=1_300_000, transcendentals=0),
    )(assignment.reshape(-1), pre, new, rq)
    return pre, new.reshape(NB, 2, ROWS, N), kept.reshape(1, 1, 2, N, N)


def solution(mesh):
    placed = (P("dp", None, "owner", None), P("dp", None, "owner", None), P())
    return jax.shard_map(
        shards,
        mesh=mesh,
        in_specs=placed,
        out_specs=(
            P("dp", "owner", None),
            P("dp", None, "owner", None),
            P("dp", "owner", None, None, None),
        ),
        check_vma=False,
    )
```

```python
import jax
import jax.numpy as jnp
from jax import lax
from jax.experimental import pallas as pl
from jax.experimental.pallas import tpu as pltpu
from jax.sharding import PartitionSpec as P

MESH = pl.DeviceIdType.MESH
F32, BF16, I16, I32 = jnp.float32, jnp.bfloat16, jnp.int16, jnp.int32
NX = NY = 4
NZ = 16
NB = 8
ROWS = 16
N = 256
H = 128
ITERS = 7
LEVELS = 32760.0 / 32768.0
B_MSG, C_MSG, G_MSG, R_MSG = 17, 9, 17, 18
G_PARTS = ((0, 6), (6, 6), (12, 5))
R_PARTS = ((0, 6), (6, 6), (12, 6))


def code(x):
    return jnp.round(x).astype(I32).astype(I16)


def encode(halves, dst):
    left, right = halves
    m = left.shape[0]
    top = jnp.maximum(jnp.max(jnp.abs(left), axis=0), jnp.max(jnp.abs(right), axis=0))
    e = jnp.ceil(jnp.log2(jnp.maximum(top, 1e-30)))
    up = (jnp.exp2(15.0 - e) * LEVELS)[None]
    dst[0:m] = code(left * up)
    dst[m : 2 * m] = code(right * up)
    dst[2 * m] = code(e)


def value(q):
    return q.astype(I32).astype(F32)


def unit(e):
    return jnp.exp2(value(e) - 15.0) * (1.0 / LEVELS)


def decode(src, m):
    down = unit(src[2 * m])[None]
    return value(src[0:m]) * down, value(src[m : 2 * m]) * down


def square_iota():
    return lax.broadcasted_iota(I32, (H, H), 0), lax.broadcasted_iota(I32, (H, H), 1)


def encode_root(x, dst):
    row, col = square_iota()
    last = x[H:, H:]
    folded = jnp.where(row <= col, x[:H, :H], last)
    diagonal = jnp.sum(jnp.where(row == col, last, 0.0), axis=0, keepdims=True)
    diagonal = jnp.where(row[:ROWS] == 0, diagonal, 0.0)
    x = jnp.concatenate([folded, x[:H, H:], diagonal], axis=0).reshape(17, ROWS, H)
    e = jnp.ceil(jnp.log2(jnp.maximum(jnp.max(jnp.abs(x), axis=0), 1e-30)))
    dst[0:17] = code(x * (jnp.exp2(15.0 - e) * LEVELS)[None])
    dst[17] = code(e)


def decode_root(q):
    v = value(q[0:17]) * unit(q[17])[None]
    folded, upper, diagonal = v[0:8].reshape(H, H), v[8:16].reshape(H, H), v[16][0:1]
    row, col = square_iota()
    turned = folded.T
    return (
        jnp.where(row <= col, folded, turned),
        upper,
        jnp.where(row > col, folded, jnp.where(row == col, diagonal, turned)),
    )


def split(x):
    high = x.astype(BF16)
    return high, (x - high.astype(F32)).astype(BF16)


def dot(a, b):
    return jnp.dot(a, b, preferred_element_type=F32)


def dot_nt(a, b):
    return lax.dot_general(a, b, (((1,), (1,)), ((), ())), preferred_element_type=F32)


def dot3(a, b):
    (ah, al), (bh, bl) = a, b
    return dot(ah, bh) + (dot(al, bh) + dot(ah, bl))


def kernel(
    p_ref, s_ref, pre_ref, new_ref, rq,
    srows, own, theirs, other, bsend, brecv, csend, crecv, gown, smat, cur, root, gq, ghi, glo,
    own_sem, their_sem, stat_sem, a_send, a_recv, b_send, b_recv, c_send, c_recv, s_send, s_recv,
    g_right, g_left, g_recv, r_right, r_left, r_recv,
):
    dp = lax.axis_index("dp")
    z = lax.axis_index("owner")
    core = lax.rem(dp, 2)
    x = lax.rem(dp // 2, NX)
    y = dp // (2 * NX)

    def plane(yy, xx, cc):
        return ((yy * NX + xx) * 2 + cc, z)

    def column(zz):
        return (dp, zz)

    def step(i, k, n):
        return lax.rem(i + k, n)

    partner = plane(y, x, 1 - core)

    def along(half, k):
        return plane(y, step(x, k, NX), core) if half == 0 else plane(step(y, k, NY), x, core)

    barrier = pltpu.get_barrier_semaphore()
    for k in range(1, NZ):
        pl.semaphore_signal(barrier, inc=1, device_id=column(step(z, k, NZ)), device_id_type=MESH)
    pl.semaphore_signal(barrier, inc=1, device_id=partner, device_id_type=MESH)
    for half in range(2):
        for k in range(1, 4):
            pl.semaphore_signal(barrier, inc=1, device_id=along(half, k), device_id_type=MESH)

    def remote(src, dst, send, recv, to):
        return pltpu.make_async_remote_copy(
            src_ref=src, dst_ref=dst, send_sem=send, recv_sem=recv, device_id=to, device_id_type=MESH
        )

    def chunk(half, k, cc):
        if half == 0:
            return p_ref.at[:, step(x, k, NX), cc, pl.ds(0, 4)]
        return p_ref.at[step(y, k, NY), :, cc, pl.ds(4, 4)]

    def to_partner(half, k):
        return remote(theirs.at[half, k], other.at[half, k], a_send.at[half, k], a_recv.at[half, k], partner)

    def load(half, k, cc, dst, sem):
        return pltpu.make_async_copy(chunk(half, k, cc), dst.at[half, k], sem.at[half, k])

    def load_mine(half, k):
        return load(half, k, core, own, own_sem)

    def load_theirs(half, k):
        return load(half, k, 1 - core, theirs, their_sem)

    def rows(k, source, to, run):
        at = column(step(z, k, NZ))
        whole = lax.rem(source // 8 + to, 2) == 0
        part = pl.ds(pl.multiple_of((source // 8) * H, H), H)

        @pl.when(whole)
        def _():
            run(remote(s_ref.at[to], smat.at[source], s_send.at[k], s_recv.at[k], at))

        @pl.when(jnp.logical_not(whole))
        def _():
            run(remote(s_ref.at[to, :, part], smat.at[source, :, part], s_send.at[k], s_recv.at[k], at))

    def rows_to(k, run):
        rows(k, z, step(z, k, NZ), run)

    def rows_from(k, run):
        rows(k, step(z, NZ - k, NZ), z, run)

    ORDER = (2, 1, 3, 0)

    def halves_of(ref, half, k, first, count):
        at = ref.at[half, k, pl.ds(first, count)]
        return tuple(at[:, :, :, i : i + H].reshape(count * 4, ROWS, H) for i in (0, H))

    def put(ref, half, k, first, count, halves):
        at = ref.at[half, k, pl.ds(first, count)]
        at[:, :, :, :H] = halves[0].reshape(count, 4, ROWS, H)
        at[:, :, :, H:] = halves[1].reshape(count, 4, ROWS, H)

    def plus(*terms):
        return tuple(sum(t[1:], t[0]) for t in zip(*terms))

    for k in ORDER:
        for half in range(2):
            load_theirs(half, k).start()
    for k in ORDER:
        for half in range(2):
            load_mine(half, k).start()
    pl.semaphore_wait(barrier, NZ - 1 + 1 + 6)
    def send_share(k):
        for half in range(2):
            load_theirs(half, k).wait()
            to_partner(half, k).start()

    send_share(2)
    for k in (8, 7, 9, 6, 10, 5, 11, 4, 12, 3, 13, 2, 14, 1, 15):
        rows_to(k, lambda c: c.start())
    for k in ORDER[1:]:
        send_share(k)
    own_rows = pltpu.make_async_copy(s_ref.at[z], smat.at[z], s_recv.at[0])
    own_rows.start()
    all_rows = pltpu.make_async_copy(s_ref, srows, stat_sem)
    all_rows.start()

    def b_copy(kind, half, d):
        at = (kind, half, d)
        return remote(bsend.at[at], brecv.at[at], b_send.at[at], b_recv.at[at], along(half, 1 + 2 * d))

    def b_start(kind, half, d, halves):
        encode(halves, bsend.at[kind, half, d])
        b_copy(kind, half, d).start()

    def b_get(kind, half, d):
        b_copy(kind, half, d).wait_recv()
        return decode(brecv.at[kind, half, d], 8)

    def c_copy(half, k):
        return remote(csend.at[half, k - 1], crecv.at[half, k - 1], c_send.at[half, k - 1], c_recv.at[half, k - 1], along(1 - half, k))

    for k in ORDER:
        for half in range(2):
            to_partner(half, k).wait_recv()
            load_mine(half, k).wait()
            total = plus(halves_of(own, half, k, 0, 4), halves_of(other, half, k, 0, 4))
            low, high = tuple(t[:8] for t in total), tuple(t[8:] for t in total)
            if k == 2:
                b_start(0, half, 0, low)
                b_start(0, half, 1, high)
            elif k == 1:
                b_start(1, half, 0, high)
                put(own, half, 1, 0, 2, low)
            elif k == 3:
                b_start(1, half, 1, low)
                put(own, half, 3, 2, 2, high)
            else:
                put(own, half, 0, 0, 4, total)
    for half in range(2):
        b_start(2, half, 0, plus(halves_of(own, half, 1, 0, 2), b_get(0, half, 0)))
        b_start(2, half, 1, plus(halves_of(own, half, 3, 2, 2), b_get(0, half, 1)))

    right_z, left_z = column(step(z, 1, NZ)), column(step(z, NZ - 1, NZ))

    def ring(buf, parts, right_sem, left_sem, recv):
        def hop(d, s, p):
            origin = step(z, NZ - s, NZ) if d == 0 else step(z, s, NZ)
            at = buf.at[origin, pl.ds(*parts[p])]
            sem = (right_sem if d == 0 else left_sem).at[s % 8, p]
            return remote(at, at, sem, recv.at[origin, p], right_z if d == 0 else left_z)

        def arrive(d, s, p):
            if s < 8 or p // 2 == d:
                c = hop(d, s, p)
                c.wait_recv()
                if s < 7 or (s == 7 and p // 2 == d):
                    c.start()

        def begin():
            for p in range(3):
                for d in range(2):
                    hop(d, 0, p).start()

        def finish(steps):
            for s in steps:
                for p in range(3):
                    for d in range(2):
                        if s < 7 or p // 2 == d:
                            hop(d, s, p).wait_send()

        return arrive, begin, finish

    g_arrive, g_begin, g_finish = ring(gq, G_PARTS, g_right, g_left, g_recv)
    r_arrive, r_begin, r_finish = ring(rq, R_PARTS, r_right, r_left, r_recv)

    def unpack_g(origin):
        a, b = decode(gq.at[origin], NB)
        ah, al = split(a)
        bh, bl = split(b)
        ghi[origin, :, :, :H] = ah
        ghi[origin, :, :, H:] = bh
        glo[origin, :, :, :H] = al
        glo[origin, :, :, H:] = bl

    def plane_sums():
        for half in range(2):
            put(own, half, 0, 0, 2, plus(halves_of(own, half, 0, 0, 2), b_get(1, half, 1), b_get(2, half, 0)))
            put(own, half, 0, 2, 2, plus(halves_of(own, half, 0, 2, 2), b_get(1, half, 0), b_get(2, half, 1)))
            me = y if half == 0 else x
            for k in (2, 1, 3):
                encode(halves_of(own, half, 0, step(me, k, 4), 1), csend.at[half, k - 1])
                c_copy(half, k).start()

    def own_sums():
        for half in range(2):
            me = y if half == 0 else x
            total = halves_of(own, half, 0, me, 1)
            for k in (1, 3, 2):
                c_copy(half, k).wait_recv()
                total = plus(total, decode(crecv.at[half, k - 1], 4))
            gown[pl.ds(4 * half, 4), :, :H], gown[pl.ds(4 * half, 4), :, H:] = total
        encode((gown[:, :, :H], gown[:, :, H:]), gq.at[z])

    def g_step(s):
        for p in range(3):
            g_arrive(0, s, p)
            g_arrive(1, s, p)

    def unpack_step(s):
        unpack_g(step(z, NZ - s, NZ))
        if s < 8:
            unpack_g(step(z, s, NZ))

    def iteration():
        current = cur[...]
        f = factor_of(current)
        fs, rs = split(f), split(root[...])
        both = tuple(jnp.concatenate([u, v], axis=0) for u, v in zip(fs, rs))
        product = dot3(both, fs)
        root[...] = product[N:]
        cur[...] = powered(fs, product[:N], current)

    own_rows.wait()
    for k in range(1, NZ):
        rows_from(k, lambda c: c.wait_recv())

    @pl.when(lax.rem(z, 2) == 0)
    def _():
        smat[8:16, :, :H] = smat[0:8, :, H:].reshape(H, H).T.reshape(8, ROWS, H)

    @pl.when(lax.rem(z, 2) == 1)
    def _():
        smat[0:8, :, H:] = smat[8:16, :, :H].reshape(H, H).T.reshape(8, ROWS, H)

    eye = (lax.broadcasted_iota(I32, (N, N), 0) == lax.broadcasted_iota(I32, (N, N), 1)).astype(F32)

    def factor_of(current):
        return (5.0 * eye - current) * 0.25

    def powered(f, square, current):
        s = split(square)
        q = dot3(s, s)
        return dot3(split(q), split(current))

    matrix = smat[...].reshape(N, N)
    magnitude = jnp.sqrt(jnp.sum(matrix * matrix, keepdims=True) + 1e-6)
    current = matrix / magnitude
    f = factor_of(current)
    root[...] = f * lax.rsqrt(jnp.sqrt(magnitude))
    fs = split(f)
    cur[...] = powered(fs, dot3(fs, fs), current)

    plane_sums()
    iteration()
    own_sums()
    g_begin()
    iteration()
    iteration()
    g_step(1)
    iteration()
    iteration()
    g_step(2)
    last = dot3(split(root[...]), split(factor_of(cur[...])))
    encode_root(last, rq.at[z])
    r_begin()

    def r_step(s, *units):
        units = units + (None,) * 6
        for i, (p, d) in enumerate(((0, 0), (0, 1), (1, 0), (1, 1), (2, 0), (2, 1))):
            r_arrive(d, s, p)
            if units[i] is not None:
                units[i]()

    def early_sends():
        for half in range(2):
            for k in range(4):
                to_partner(half, k).wait_send()
            for kind in range(3):
                for d in range(2):
                    b_copy(kind, half, d).wait_send()
            for k in range(1, 4):
                c_copy(half, k).wait_send()
        for k in range(1, NZ):
            rows_to(k, lambda c: c.wait_send())

    unpack_g(z)
    unpack_step(1)
    for s in range(1, 6):
        g_step(s + 2)
        unpack_step(s + 1)
        r_step(s)
        if s == 2:
            early_sends()
    g_step(8)
    unpack_step(7)
    unpack_step(8)
    all_rows.wait()

    pick = (
        lax.broadcasted_iota(I32, (ROWS, N), 1) == lax.broadcasted_iota(I32, (ROWS, N), 0) + z * ROWS
    ).astype(F32).astype(BF16)

    def halves(b):
        return ghi[:, b].reshape(N, N), glo[:, b].reshape(N, N)

    def statistics(b):
        gh, gl = halves(b)
        rh, rl = split(gown[b])
        one = dot_nt(jnp.concatenate([rh, rl, pick], axis=0), gh)
        two = dot_nt(jnp.concatenate([rh, pick], axis=0), gl)
        new_ref[2 * b] = srows[2 * b] + one[:16] + (one[16:32] + two[:16])
        ch, cl = one[32:48].astype(BF16), two[16:32].astype(BF16)
        three = dot(jnp.concatenate([ch, cl], axis=0), gh)
        new_ref[2 * b + 1] = srows[2 * b + 1] + three[:16] + (three[16:32] + dot(ch, gl))

    z8 = lax.rem(z, 8)
    line = lax.broadcasted_iota(I32, (ROWS, H), 0) + z8 * ROWS
    lane = lax.broadcasted_iota(I32, (ROWS, H), 1)
    pick_in = (lane == line).astype(F32).astype(BF16)

    def precondition(t):
        b = step(pair, t, NB)
        gh, gl = halves(b)
        q = rq[2 * b]
        down = unit(q[17])
        high, low = split((value(q[0:16]) * down[None]).reshape(2 * H, H))
        turned = dot_nt(pick_in, high) + dot_nt(pick_in, low)
        folded = value(rq[2 * b, z8]) * down
        upper = value(rq[2 * b, 8 + z8]) * down
        diagonal = (value(q[16]) * down)[0:1]
        first = jnp.concatenate([jnp.where(line <= lane, folded, turned[:, :H]), upper], axis=1)
        second = jnp.where(line > lane, folded, jnp.where(line == lane, diagonal, turned[:, :H]))
        rows = jnp.where(z < 8, first, jnp.concatenate([turned[:, H:], second], axis=1))
        lh, ll = split(rows)
        shaped = dot(jnp.concatenate([lh, ll], axis=0), gh)
        shaped = shaped[:16] + (shaped[16:] + dot(lh, gl))
        a, c, d = decode_root(rq[2 * b + 1])
        right = jnp.concatenate(
            [jnp.concatenate([a, c], axis=1), jnp.concatenate([c.T, d], axis=1)], axis=0
        )
        rh, rl = split(right)
        sh, sl = split(shaped)
        out = dot(jnp.concatenate([sh, sl], axis=0), rh)
        pre_ref[b] = out[:16] + (out[16:] + dot(sh, rl))

    pair = z // 2

    def stat(b):
        return lambda: statistics(b)

    def pre(t):
        return lambda: precondition(t)

    r_step(6, stat(0), stat(1), stat(2), stat(3))
    r_step(7, stat(4), stat(5), stat(6), stat(7))
    for t in (0, 1, 7, 2, 6, 3, 5):
        precondition(t)
    g_finish(range(8))
    r_finish(range(6))
    r_step(8)
    precondition(4)
    r_finish((6, 7))


def output_kernel(owner_ref, pre_in, new_in, rq, pre_ref, new_ref, kept_ref, sem):
    dp = lax.axis_index("dp")
    z = lax.axis_index("owner")
    copies = [
        pltpu.make_async_copy(src, dst, sem.at[i])
        for i, (src, dst) in enumerate(((pre_in, pre_ref), (new_in, new_ref)))
    ]
    for copy in copies:
        copy.start()

    first, second, count = jnp.int32(0), jnp.int32(0), jnp.int32(0)
    for j in range(16):
        hit = owner_ref[dp * 16 + j] == z
        first = jnp.where(hit & (count == 0), j, first)
        second = jnp.where(hit & (count == 1), j, second)
        count = count + hit.astype(I32)
    for slot, j in enumerate((first, second)):
        live = (count > slot).astype(F32)
        a, c, d = decode_root(rq[j])
        kept_ref[slot, 0:8, :, :H] = (a * live).astype(BF16).reshape(8, ROWS, H)
        kept_ref[slot, 0:8, :, H:] = (c * live).astype(BF16).reshape(8, ROWS, H)
        kept_ref[slot, 8:16, :, :H] = (c.T * live).astype(BF16).reshape(8, ROWS, H)
        kept_ref[slot, 8:16, :, H:] = (d * live).astype(BF16).reshape(8, ROWS, H)

    for copy in copies:
        copy.wait()


def shards(partials, statistics, assignment):
    vmem, dma = pltpu.VMEM, pltpu.SemaphoreType.DMA
    in_vmem, in_hbm = pl.BlockSpec(memory_space=pltpu.VMEM), pl.BlockSpec(memory_space=pl.ANY)
    shapes = (
        jax.ShapeDtypeStruct((NB, ROWS, N), F32),
        jax.ShapeDtypeStruct((2 * NB, ROWS, N), F32),
    )
    pre, new, rq = pl.pallas_call(
        kernel,
        out_shape=(*shapes, jax.ShapeDtypeStruct((NZ, R_MSG, ROWS, H), I16)),
        in_specs=[in_hbm] * 2,
        out_specs=[in_vmem] * 3,
        scratch_shapes=[
            vmem((2 * NB, ROWS, N), F32),
            vmem((2, 4, 4, 4, ROWS, N), F32),
            vmem((2, 4, 4, 4, ROWS, N), F32),
            vmem((2, 4, 4, 4, ROWS, N), F32),
            vmem((3, 2, 2, B_MSG, ROWS, H), I16),
            vmem((3, 2, 2, B_MSG, ROWS, H), I16),
            vmem((2, 3, C_MSG, ROWS, H), I16),
            vmem((2, 3, C_MSG, ROWS, H), I16),
            vmem((NB, ROWS, N), F32),
            vmem((NZ, ROWS, N), F32),
            vmem((N, N), F32),
            vmem((N, N), F32),
            vmem((NZ, G_MSG, ROWS, H), I16),
            vmem((NZ, NB, ROWS, N), BF16),
            vmem((NZ, NB, ROWS, N), BF16),
            dma((2, 4)), dma((2, 4)), dma, dma((2, 4)), dma((2, 4)),
            dma((3, 2, 2)), dma((3, 2, 2)), dma((2, 3)), dma((2, 3)),
            dma((NZ,)), dma((NZ,)),
            dma((8, 3)), dma((8, 3)), dma((NZ, 3)),
            dma((8, 3)), dma((8, 3)), dma((NZ, 3)),
        ],
        compiler_params=pltpu.CompilerParams(
            collective_id=0, has_side_effects=True, vmem_limit_bytes=50 * 1024 * 1024
        ),
        cost_estimate=pl.CostEstimate(flops=3_000_000_000, bytes_accessed=6_000_000, transcendentals=0),
    )(partials.reshape(NY, NX, 2, NB, ROWS, N), statistics.reshape(2 * NB, ROWS, N))
    pre, new, kept = pl.pallas_call(
        output_kernel,
        out_shape=(*shapes, jax.ShapeDtypeStruct((2, 16, 16, N), BF16)),
        in_specs=[pl.BlockSpec(memory_space=pltpu.SMEM)] + [in_vmem] * 3,
        out_specs=[in_hbm, in_hbm, in_vmem],
        scratch_shapes=[dma((2,))],
        compiler_params=pltpu.CompilerParams(vmem_limit_bytes=32 * 1024 * 1024),
        cost_estimate=pl.CostEstimate(flops=1_000_000, bytes_accessed=1_300_000, transcendentals=0),
    )(assignment.reshape(-1), pre, new, rq)
    return pre, new.reshape(NB, 2, ROWS, N), kept.reshape(1, 1, 2, N, N)


def solution(mesh):
    placed = (P("dp", None, "owner", None), P("dp", None, "owner", None), P())
    return jax.shard_map(
        shards,
        mesh=mesh,
        in_specs=placed,
        out_specs=(
            P("dp", "owner", None),
            P("dp", None, "owner", None),
            P("dp", "owner", None, None, None),
        ),
        check_vma=False,
    )
```
